256 devices in a mesh: dp: 4 (over x), expert: 8 (over z), etp: 8 (over y, core).
Axes of the slice: x: 4, y: 4, z: 8, core: 2. Of those that a mesh axis runs over, the one named last changes fastest.
Arguments:
- grad_output: bfloat16 [2048, 6144], P(('dp', 'expert', 'etp')), may hold values from -6 to 6
- comb_weights: bfloat16 [2048, 4], P(('dp', 'expert', 'etp')), may hold values from 0.099609375 to 1
- expert_ids: int32 [2048, 4], P(('dp', 'expert', 'etp')), may hold values from 0 to 7, all different within a row; in each aligned block of 8 rows (0 to 7, 8 to 15, ...) at most 6 rows name the same one
- down_weight: bfloat16 [8, 6144, 6144], P('expert', 'etp', 'dp'), may hold values from -0.078125 to 0.078125
- gate_weight: bfloat16 [8, 6144, 6144], P('expert', 'dp', 'etp'), may hold values from -0.078125 to 0.078125
- up_weight: bfloat16 [8, 6144, 6144], P('expert', 'dp', 'etp'), may hold values from -0.078125 to 0.078125
- gate_saved: bfloat16 [8, 1536, 6144], P('expert', None, 'etp'), may hold values from -6 to 6
- up_saved: bfloat16 [8, 1536, 6144], P('expert', None, 'etp'), may hold values from -6 to 6
Outputs:
- input_grad: bfloat16 [2048, 6144], P(('dp', 'expert', 'etp'))
The draws below stay inside these ranges and needn't reach their ends.
Inputs may be any that keep to these rules, and one draw needn't show every extreme that they name: `expert_ids`: each token names 4 different experts; no expert is named by more than 6 of the tokens of one device.
All inputs are finite; a program needn't handle non-finite values.
Results may differ from the reference program's by a relative error of at most 0.0049.
Values may be sent and summed in bfloat16 or wider, within the bound.
A program may use at most 128 MiB of HBM per device.

```python
import math
import jax
import jax.numpy as jnp
import numpy as np
from jax import lax

D = 6144
FF = 6144
TOP = 4
TOK_DEV = 8
EXPERTS = 8
CAP = 6
TOKENS = 2048
SLOTS = 1536
N_DP = 4
N_EXPERT = 8
N_ETP = 8


def levels(own_key, shape, cuts, smallest, largest):
    level = 1.0
    for dim, shards_of in cuts:
        draws = jax.random.uniform(jax.random.fold_in(jax.random.fold_in(own_key, 6), dim), (shards_of,), jnp.float32, smallest / len(cuts), largest / len(cuts))
        level = level * jnp.repeat(jnp.exp(draws), shape[dim] // shards_of).reshape((-1,) + (1,) * (len(shape) - 1 - dim))
    return level


def assign_block(stream_key, own, number, rows, amount, top, most, slope):
    ranking = jax.random.permutation(stream_key, amount)
    packed, common = shares(amount, rows * top, most, slope, True), shares(amount, rows * top, most, slope, False)
    places = jnp.arange(amount)

    def named(tallies, rotation):
        used = int((tallies > 0).sum())
        fixed = max(1, used // 4)
        shifted = fixed + (places - fixed + rotation * (used - fixed)) % max(1, amount - fixed)
        return jnp.zeros((amount,), jnp.int32).at[ranking[jnp.where(places < fixed, places, shifted)]].set(jnp.asarray(tallies, jnp.int32))

    tallies = jnp.where(number % 4 == 0, named(packed, number // 4), named(common, number - number // 4 - 1))
    mixed = jax.random.permutation(jax.random.fold_in(own, 3), amount)
    donor, receiver = mixed[0:amount // 2 * 2:2], mixed[1:amount // 2 * 2:2]
    room = jnp.minimum(tallies[donor] - 1, most - tallies[receiver]) // 2
    room = jnp.where((donor == ranking[0]) | (receiver == ranking[0]) | (tallies[receiver] == 0), 0, jnp.maximum(room, 0))
    shifted = jax.random.randint(jax.random.fold_in(own, 4), (amount // 2,), 0, 1 << 20) % (room + 1)
    tallies = tallies.at[donor].add(-shifted).at[receiver].add(shifted)
    members = jnp.searchsorted(jnp.cumsum(tallies), jnp.arange(rows * top), side="right").astype(jnp.int32)
    grid = members.reshape(top, rows).T
    grid = grid[jax.random.permutation(jax.random.fold_in(own, 1), rows)]
    rotation = jax.random.randint(jax.random.fold_in(own, 2), (rows, 1), 0, top)
    return jnp.take_along_axis(grid, (jnp.arange(top)[None, :] + rotation) % top, axis=1)


def shares(amount, total, bound, slope, full):
    weights = [(1 << 20) // math.isqrt(rank ** slope) + 1 for rank in range(1, amount + 1)]
    largest = bound if full else min(bound, max(-(-total // amount), total * weights[0] // sum(weights)))
    least = 1 if total - largest >= amount - 1 else 0
    counts, surplus = [largest] + [least] * (amount - 1), total - largest - least * (amount - 1)
    while surplus > 0:
        candidates = [i for i in range(1, amount) if counts[i] < largest] or [i for i in range(1, amount) if counts[i] < bound]
        whole, left = sum([weights[i] for i in candidates]), surplus
        for i in candidates:
            extra = min(bound - counts[i], max(1, left * weights[i] // whole), surplus)
            counts[i] = counts[i] + extra
            surplus = surplus - extra
    return np.array(counts)


def centred(rng, extent, spread, limit, shards=(), kind=jnp.bfloat16):
    values = jax.random.normal(rng, extent, jnp.float32) * spread
    if len(shards) > 0:
        values = levels(rng, extent, shards, -0.22, 0.18) * values
    return jnp.clip(values, min=-limit, max=limit).astype(kind)


def setup_inputs(seed: int = 0) -> dict:
    splits = jax.random.split(jax.random.key(seed), 9)
    grad_output = centred(splits[0], (TOKENS, D), 1.0, 6.0, ((0, 256),))
    comb_weights = jnp.clip(0.099609375 + 0.9003906 * jax.random.uniform(splits[1], (TOKENS, TOP), jnp.float32) ** levels(splits[1], (TOKENS, TOP), ((0, 256),), -0.2, 0.2), 0.099609375, 1.0).astype(jnp.bfloat16)
    expert_ids_keys = jax.random.split(jax.random.fold_in(splits[2], 1), TOKENS // TOK_DEV)
    expert_ids_turns = jax.random.permutation(jax.random.fold_in(splits[2], 3), TOKENS // TOK_DEV)
    expert_ids = jax.vmap(lambda own, number: assign_block(jax.random.fold_in(splits[2], 2), own, number, TOK_DEV, EXPERTS, TOP, CAP, 2))(expert_ids_keys, expert_ids_turns).reshape((TOKENS, TOP))
    down_weight = centred(splits[3], (EXPERTS, FF, D), FF ** -0.5, 0.078125, ((0, 8), (1, 8), (2, 4)))
    gate_weight = centred(splits[4], (EXPERTS, D, FF), D ** -0.5, 0.078125, ((0, 8), (1, 4), (2, 8)))
    up_weight = centred(splits[5], (EXPERTS, D, FF), D ** -0.5, 0.078125, ((0, 8), (1, 4), (2, 8)))
    gate_saved = centred(splits[6], (EXPERTS, SLOTS, FF), 1.0, 6.0, ((0, 8), (2, 8)))
    up_saved = centred(splits[7], (EXPERTS, SLOTS, FF), 1.0, 6.0, ((0, 8), (2, 8)))
    return {"grad_output": grad_output, "comb_weights": comb_weights, "expert_ids": expert_ids, "down_weight": down_weight, "gate_weight": gate_weight, "up_weight": up_weight, "gate_saved": gate_saved, "up_saved": up_saved}


def swiglu_backward(hidden_raw, weight, gate_pre, up_pre):
    gate_value = gate_pre.astype(jnp.float32)
    up_value = up_pre.astype(jnp.float32)
    sigmoid_gate = jax.nn.sigmoid(gate_value)
    scaled = hidden_raw * weight[:, None]
    gate_grad = (scaled * up_value * sigmoid_gate * (1.0 + gate_value * (1.0 - sigmoid_gate))).astype(jnp.bfloat16)
    up_grad = (scaled * gate_value * sigmoid_gate).astype(jnp.bfloat16)
    return gate_grad, up_grad


def reference(grad_output, comb_weights, expert_ids, down_weight, gate_weight, up_weight, gate_saved, up_saved):
    block_count = TOKENS // TOK_DEV
    labels = jnp.arange(EXPERTS, dtype=jnp.int32)
    block_ids = expert_ids.reshape(block_count, TOK_DEV, TOP)
    matches = (block_ids[:, :, :, None] == labels[None, None, None, :]).astype(jnp.int32)
    expert_hits = jnp.sum(matches, axis=2)
    before = jnp.cumsum(expert_hits, axis=1) - expert_hits
    position = jnp.sum(matches * before[:, :, None, :], axis=3)
    block_index = jnp.arange(block_count, dtype=jnp.int32)
    group_index = block_index // (N_EXPERT * N_ETP)
    expert_source = (block_index // N_ETP) % N_EXPERT
    tensor_source = block_index % N_ETP
    slot_base = ((expert_source * N_ETP + tensor_source) * N_DP + group_index) * CAP
    slot = (slot_base[:, None, None] + position).reshape(TOKENS, TOP).astype(jnp.int32)
    token_index = jnp.broadcast_to(jnp.arange(TOKENS, dtype=jnp.int32)[:, None], (TOKENS, TOP))
    routed = jnp.zeros((EXPERTS, SLOTS, D), jnp.bfloat16).at[expert_ids, slot].set(grad_output[token_index])
    slot_weight = jnp.zeros((EXPERTS, SLOTS), jnp.float32).at[expert_ids, slot].set(comb_weights.astype(jnp.float32))

    def one_expert(operands):
        routed_rows, weight, down_matrix, gate_matrix, up_matrix, gate_pre, up_pre = operands
        hidden_raw = jnp.dot(routed_rows, down_matrix.T, preferred_element_type=jnp.float32)
        gate_grad, up_grad = swiglu_backward(hidden_raw, weight, gate_pre, up_pre)
        first = jnp.dot(gate_grad, gate_matrix.T, preferred_element_type=jnp.float32)
        second = jnp.dot(up_grad, up_matrix.T, preferred_element_type=jnp.float32)
        return first + second

    slot_grad = lax.map(one_expert, (routed, slot_weight, down_weight, gate_weight, up_weight, gate_saved, up_saved))
    picked = slot_grad[expert_ids, slot]
    return jnp.sum(picked, axis=1).astype(jnp.bfloat16)
```

```python
import jax
import jax.numpy as jnp
from jax import lax
from jax.experimental import pallas as pl
from jax.experimental.pallas import tpu as pltpu
from jax.sharding import PartitionSpec as P

MESH = pl.DeviceIdType.MESH
NX, NZ, NT, NY = 4, 8, 8, 4
CAP = 6
ROWS = NX * CAP
BLOCK = 2 * ROWS
META = 128
CHUNKS = ((1, -1), (2, -2), (3, -3), (4, 0))
SKEW = 3
F32, BF16 = jnp.float32, jnp.bfloat16


def dot_nt(a, b):
    return lax.dot_general(a, b, (((1,), (1,)), ((), ())), preferred_element_type=F32)


def aligned(start, unit):
    return pl.multiple_of(start * unit, unit)


def kernel(
    tok, dw_hbm, gw_hbm, uw_hbm, gs_hbm, us_hbm, out,
    dw, gw, uw, gs, us, t2, rows, hp32, hp, xo, xl, xr, hf, gg, ug, sg, yb, pb, yo, yl, yr, zs, zr, fin, fr,
    load_sem, send_sem, recv_sem,
):
    d, e, t = lax.axis_index("dp"), lax.axis_index("expert"), lax.axis_index("etp")
    y, c = lax.div(t, 2), lax.rem(t, 2)
    fh = tok.shape[1] - META
    fq = 2 * fh
    fe = dw.shape[0]
    quarter = 2 * BLOCK

    loads = []
    for i, (src, dst) in enumerate(
        ((dw_hbm, dw), (gs_hbm, gs), (us_hbm, us), (gw_hbm, gw), (uw_hbm, uw))
    ):
        loads.append(pltpu.make_async_copy(src, dst, load_sem.at[i]))
        loads[-1].start()

    def at_x(j):
        return (lax.rem(d + j + NX, NX), e, t)

    def at_y(j):
        return (d, e, 2 * lax.rem(y + j + NY, NY) + c)

    def at_z(j):
        return (d, lax.rem(e + j + NZ, NZ), t)

    sibling = (d, e, 2 * y + 1 - c)

    barrier = pltpu.get_barrier_semaphore()
    partners = [at_x(j) for j in range(1, NX)] + [at_z(j) for j in range(1, NZ)]
    partners += [at_y(1), at_y(-1), sibling]
    for device in partners:
        pl.semaphore_signal(barrier, inc=1, device_id=device, device_id_type=MESH)
    pl.semaphore_wait(barrier, len(partners))

    sent = []

    def send(src, dst, device):
        i = len(sent)
        copy = pltpu.make_async_remote_copy(
            src_ref=src,
            dst_ref=dst,
            send_sem=send_sem.at[i],
            recv_sem=recv_sem.at[i],
            device_id=device,
            device_id_type=MESH,
        )
        copy.start()
        sent.append(copy)
        return copy

    here = pl.ds(aligned(d, 16), 16)
    first = []
    for j in range(1, NX):
        there = pl.ds(aligned(lax.rem(d + j, NX), 16), 16)
        first.append(send(tok.at[there, :], t2.at[0, here, :], at_x(j)))
    t2[0, here, :] = tok[here, :]
    for copy in first:
        copy.wait_recv()
    gather = {
        1: send(t2.at[0], t2.at[1], at_z(-1)),
        -1: send(t2.at[0], t2.at[NZ - 1], at_z(1)),
    }

    def meta_of(r):
        return sum(
            t2[r % NZ, g * 16 : (g + 1) * 16, fh : fh + META].astype(F32) for g in range(NX)
        )

    def meta_row(meta, row):
        ids = lax.broadcasted_iota(jnp.int32, meta.shape, 0)
        return jnp.sum(jnp.where(ids == row, meta, 0.0), axis=0, keepdims=True)[:, :64]

    slot = lax.broadcasted_iota(jnp.int32, (ROWS, 64), 0)
    lane = lax.broadcasted_iota(jnp.int32, (ROWS, 64), 1)
    group = (
        (slot >= CAP).astype(jnp.int32)
        + (slot >= 2 * CAP).astype(jnp.int32)
        + (slot >= 3 * CAP).astype(jnp.int32)
    )
    place = (slot - CAP * group + 1).astype(F32)
    same_group = (lane >> 4) == group
    half_of_lane = (lane >> 3) & 1

    def choose(code, h):
        return same_group & (half_of_lane == h) & (code == place)

    state = [dict() for _ in CHUNKS]

    def select(k):
        for r in CHUNKS[k]:
            if r == 0:
                continue
            gather[r].wait_recv()
            if r > 0 and r < 4:
                gather[r + 1] = send(t2.at[r], t2.at[r + 1], at_z(-1))
            if r < 0 and r > -3:
                gather[r - 1] = send(t2.at[NZ + r], t2.at[NZ + r - 1], at_z(1))
        codes = [meta_row(meta_of(r), e) for r in CHUNKS[k]]
        mine = pl.ds(aligned(t, BLOCK), BLOCK)
        for h in range(2):
            parts = [
                jnp.dot(
                    choose(code, h).astype(F32).astype(BF16),
                    t2[r % NZ, :, 0:fh],
                    preferred_element_type=F32,
                )
                for code, r in zip(codes, CHUNKS[k])
            ]
            rows[k, mine, h * fh : (h + 1) * fh] = jnp.concatenate(parts, axis=0).astype(BF16)
        block = rows.at[k, mine, :]
        state[k]["ag"] = (
            send(block, block, at_y(1)),
            send(block, block, at_y(-1)),
            send(block, block, sibling),
        )

    def gather_pass(k):
        from_left, from_right, other = state[k]["ag"]
        left = pl.ds(aligned(2 * lax.rem(y + NY - 1, NY) + c, BLOCK), BLOCK)
        right = pl.ds(aligned(2 * lax.rem(y + 1, NY) + c, BLOCK), BLOCK)
        from_left.wait_recv()
        half = rows.at[k, left, 0:fh]
        a = send(half, half, at_y(1))
        whole = rows.at[k, left, :]
        sl = send(whole, whole, sibling)
        from_right.wait_recv()
        half = rows.at[k, right, fh:fq]
        b = send(half, half, at_y(-1))
        whole = rows.at[k, right, :]
        sr = send(whole, whole, sibling)
        state[k]["ag2"] = (a, b)
        state[k]["sib"] = [other, sl, sr]

    def gather_last(k):
        opposite = pl.ds(aligned(2 * lax.rem(y + 2, NY) + c, BLOCK), BLOCK)
        a, b = state[k]["ag2"]
        a.wait_recv()
        half = rows.at[k, opposite, 0:fh]
        state[k]["sib"].append(send(half, half, sibling))
        b.wait_recv()
        half = rows.at[k, opposite, fh:fq]
        state[k]["sib"].append(send(half, half, sibling))

    q_right, q_left = lax.rem(d + 1, NX), lax.rem(d + NX - 1, NX)
    q_far = lax.rem(d + 2, NX)

    def half_a(q):
        return pl.ds(pl.multiple_of(q * quarter, quarter), BLOCK)

    def half_b(q):
        return pl.ds(pl.multiple_of(q * quarter + BLOCK, BLOCK), BLOCK)

    def whole_q(q):
        return pl.ds(pl.multiple_of(q * quarter, quarter), quarter)

    def hidden(k):
        for copy in state[k]["sib"]:
            copy.wait_recv()
        if k == 0:
            loads[0].wait()
        tile = min(256, fe)

        @pl.loop(0, fe // tile)
        def _(n):
            cols = pl.ds(pl.multiple_of(n * tile, tile), tile)
            part = dot_nt(rows[k], dw[cols, :])
            hp32[k, :, cols] = part
            hp[k, :, cols] = part.astype(BF16)

        far_a = send(hp.at[k, half_a(q_far), :], xo.at[k, 0], at_x(1))
        far_b = send(hp.at[k, half_b(q_far), :], xo.at[k, 1], at_x(-1))
        near_b = send(hp.at[k, half_b(q_right), :], xl.at[k, BLOCK:quarter, :], at_x(1))
        near_a = send(hp.at[k, half_a(q_left), :], xr.at[k, 0:BLOCK, :], at_x(-1))
        state[k]["rs"] = (far_a, far_b)
        state[k]["rs2"] = [near_b, near_a]

    def reduce_pass(k):
        far_a, far_b = state[k]["rs"]
        far_a.wait_recv()
        to = half_a(q_right)
        hp[k, to, :] = (hp32[k, to, :] + xo[k, 0].astype(F32)).astype(BF16)
        state[k]["rs2"].append(send(hp.at[k, to, :], xl.at[k, 0:BLOCK, :], at_x(1)))
        far_b.wait_recv()
        to = half_b(q_left)
        hp[k, to, :] = (hp32[k, to, :] + xo[k, 1].astype(F32)).astype(BF16)
        state[k]["rs2"].append(send(hp.at[k, to, :], xr.at[k, BLOCK:quarter, :], at_x(-1)))

    def reduce_last(k):
        for copy in state[k]["rs2"]:
            copy.wait_recv()
        mine = whole_q(d)
        total = hp32[k, mine, :] + xl[k].astype(F32) + xr[k].astype(F32)
        hf[k, mine, :] = total.astype(BF16)
        block = hf.at[k, mine, :]
        state[k]["hg"] = (send(block, block, at_x(1)), send(block, block, at_x(-1)))

    def spread_pass(k):
        from_left, from_right = state[k]["hg"]
        from_left.wait_recv()
        block = hf.at[k, half_a(q_left), :]
        a = send(block, block, at_x(1))
        from_right.wait_recv()
        block = hf.at[k, half_b(q_right), :]
        b = send(block, block, at_x(-1))
        state[k]["hg2"] = (a, b)

    def slot_rows(ref, k, cols):
        pieces = []
        for r in CHUNKS[k]:
            source = lax.rem(e + r + NZ, NZ)
            start = pl.multiple_of(source * (NT * ROWS), NT * ROWS)
            pieces.append(ref[pl.ds(start, NT * ROWS), cols].astype(F32))
        return jnp.concatenate(
            [p[i * ROWS : (i + 1) * ROWS] for i in range(NT) for p in pieces], axis=0
        )

    def backward(k):
        for copy in state[k]["hg2"]:
            copy.wait_recv()
        if k == 0:
            for copy in loads[1:]:
                copy.wait()

        @pl.loop(0, fe // 128)
        def _(n):
            cols = pl.ds(pl.multiple_of(n * 128, 128), 128)
            h = hf[k, :, cols].astype(F32)
            gate = slot_rows(gs, k, cols)
            up = slot_rows(us, k, cols)
            s = jax.nn.sigmoid(gate)
            gg[:, cols] = (h * up * s * (1.0 + gate * (1.0 - s))).astype(BF16)
            ug[:, cols] = (h * gate * s).astype(BF16)

        tile = min(256, fq)

        @pl.loop(0, fq // tile)
        def _(n):
            cols = pl.ds(pl.multiple_of(n * tile, tile), tile)
            part = dot_nt(gg[...], gw[cols, :]) + dot_nt(ug[...], uw[cols, :])
            for i in range(NT):
                sg[k, i // 2, i % 2, :, cols] = part[i * BLOCK : (i + 1) * BLOCK]

        state[k]["pair"] = send(sg.at[k, :, 1 - c], yb.at[k], sibling)

    y_right, y_left, y_far = lax.rem(y + 1, NY), lax.rem(y + NY - 1, NY), lax.rem(y + 2, NY)
    low, high = slice(0, fh), slice(fh, fq)

    def pair_sum(k, q, cols):
        return sg[k, q, c, :, cols] + yb[k, q, :, cols]

    def slot_pass(k):
        state[k]["pair"].wait_recv()
        pb[k, 0] = pair_sum(k, y_far, slice(0, fq)).astype(BF16)
        far_a = send(pb.at[k, 0, :, low], yo.at[k, 0], at_y(1))
        far_b = send(pb.at[k, 0, :, high], yo.at[k, 1], at_y(-1))
        pb[k, 1, :, high] = pair_sum(k, y_right, high).astype(BF16)
        near_b = send(pb.at[k, 1, :, high], yl.at[k, :, high], at_y(1))
        pb[k, 2, :, low] = pair_sum(k, y_left, low).astype(BF16)
        near_a = send(pb.at[k, 2, :, low], yr.at[k, :, low], at_y(-1))
        state[k]["ys"] = (far_a, far_b)
        state[k]["ys2"] = [near_b, near_a]

    def slot_pass2(k):
        far_a, far_b = state[k]["ys"]
        far_a.wait_recv()
        pb[k, 1, :, low] = (pair_sum(k, y_right, low) + yo[k, 0].astype(F32)).astype(BF16)
        state[k]["ys2"].append(send(pb.at[k, 1, :, low], yl.at[k, :, low], at_y(1)))
        far_b.wait_recv()
        pb[k, 2, :, high] = (pair_sum(k, y_left, high) + yo[k, 1].astype(F32)).astype(BF16)
        state[k]["ys2"].append(send(pb.at[k, 2, :, high], yr.at[k, :, high], at_y(-1)))

    returns = []

    def slot_last(k):
        for copy in state[k]["ys2"]:
            copy.wait_recv()
        total = pair_sum(k, y, slice(0, fq)) + yl[k].astype(F32) + yr[k].astype(F32)
        for i, r in enumerate(CHUNKS[k]):
            part = total[i * ROWS : (i + 1) * ROWS]
            if r == 0:
                zr[0] = part
            else:
                zs[k, i] = part
                returns.append(send(zs.at[k, i], zr.at[(-r) % NZ], at_z(r)))

    stages = (
        select, gather_pass, gather_last, hidden, reduce_pass, reduce_last,
        spread_pass, backward, slot_pass, slot_pass2, slot_last,
    )
    for step in range(len(stages) + SKEW * (len(CHUNKS) - 1)):
        for k in range(len(CHUNKS)):
            s = step - SKEW * k
            if 0 <= s < len(stages):
                stages[s](k)

    meta = meta_of(0)
    mix = [[], []]
    for j in range(NZ):
        x = lax.rem(e + j, NZ)
        code, weight = meta_row(meta, x), meta_row(meta, x + NZ)
        for h in range(2):
            mix[h].append(jnp.where(choose(code, h), weight, 0.0))
    mix = [jnp.concatenate(m, axis=0).astype(BF16) for m in mix]
    for copy in returns:
        copy.wait_recv()

    def combine(h):
        value = zr[:, :, h * fh : (h + 1) * fh].reshape(NZ * ROWS, fh)
        coarse = value.astype(BF16)
        fine = (value - coarse.astype(F32)).astype(BF16)
        dims = (((0,), (0,)), ((), ()))
        return lax.dot_general(mix[h], coarse, dims, preferred_element_type=F32) + lax.dot_general(
            mix[h], fine, dims, preferred_element_type=F32
        )

    fin[...] = (combine(0) + combine(1)).astype(BF16)
    last = []
    for j in range(1, NX):
        there = pl.ds(aligned(lax.rem(d + j, NX), 16), 16)
        last.append(send(fin.at[there, :], fr.at[here, :], at_x(j)))
    fr[here, :] = fin[here, :]
    for copy in last:
        copy.wait_recv()
    out[...] = fr[...]
    for copy in sent:
        copy.wait_send()


COPIES = 3 + 7 + 4 * (3 + 4 + 2 + 4 + 2 + 2 + 2 + 1 + 4 + 2) + 7 + 3


def on_device(
    grad_output, comb_weights, expert_ids, down_weight, gate_weight, up_weight, gate_saved, up_saved
):
    tokens, width = grad_output.shape
    fq = width // NX
    fh = fq // 2
    fe = down_weight.shape[1]
    slots = gate_saved.shape[1]
    d = lax.axis_index("dp")
    experts = jnp.arange(NZ, dtype=jnp.int32)
    match = expert_ids[None, :, :] == experts[:, None, None]
    hits = jnp.any(match, axis=2)
    earlier = jnp.arange(tokens)[:, None] < jnp.arange(tokens)[None, :]
    before = jnp.sum(jnp.where(hits[:, :, None] & earlier[None], 1.0, 0.0), axis=1)
    code = jnp.where(hits, before + 1.0, 0.0)
    weight = jnp.sum(jnp.where(match, comb_weights.astype(F32)[None], 0.0), axis=2)
    meta = jnp.concatenate([code, weight], axis=0).astype(BF16)
    lanes = jnp.arange(META) // 16 == d
    meta = jnp.where(lanes[None, :], jnp.tile(meta, (1, META // tokens)), 0)
    value = grad_output.reshape(tokens, NX, 2, fh).transpose(1, 2, 0, 3).reshape(NX, 16, fh)
    tok = jnp.concatenate([value, jnp.broadcast_to(meta[None], (NX, 16, META))], axis=2)
    tok = tok.reshape(NX * 16, fh + META)

    n = len(CHUNKS)
    vmem = pltpu.VMEM
    any_space = pl.BlockSpec(memory_space=pl.ANY)
    in_vmem = pl.BlockSpec(memory_space=pltpu.VMEM)
    out = pl.pallas_call(
        kernel,
        out_shape=jax.ShapeDtypeStruct((NX * 16, fh), BF16),
        in_specs=[in_vmem] + [any_space] * 5,
        out_specs=in_vmem,
        scratch_shapes=[
            vmem((fe, fq), BF16),
            vmem((fq, fe), BF16),
            vmem((fq, fe), BF16),
            vmem((slots, fe), BF16),
            vmem((slots, fe), BF16),
            vmem((NZ, 64, fh + META), BF16),
            vmem((n, NT * BLOCK, fq), BF16),
            vmem((n, NT * BLOCK, fe), F32),
            vmem((n, NT * BLOCK, fe), BF16),
            vmem((n, 2, BLOCK, fe), BF16),
            vmem((n, 2 * BLOCK, fe), BF16),
            vmem((n, 2 * BLOCK, fe), BF16),
            vmem((n, NT * BLOCK, fe), BF16),
            vmem((NT * BLOCK, fe), BF16),
            vmem((NT * BLOCK, fe), BF16),
            vmem((n, NY, 2, BLOCK, fq), F32),
            vmem((n, NY, BLOCK, fq), F32),
            vmem((n, 3, BLOCK, fq), BF16),
            vmem((n, 2, BLOCK, fh), BF16),
            vmem((n, BLOCK, fq), BF16),
            vmem((n, BLOCK, fq), BF16),
            vmem((n, 2, ROWS, fq), F32),
            vmem((NZ, ROWS, fq), F32),
            vmem((64, fh), BF16),
            vmem((64, fh), BF16),
            pltpu.SemaphoreType.DMA((5,)),
            pltpu.SemaphoreType.DMA((COPIES,)),
            pltpu.SemaphoreType.DMA((COPIES,)),
        ],
        compiler_params=pltpu.CompilerParams(
            collective_id=0, has_side_effects=True, vmem_limit_bytes=58 * 1024 * 1024
        ),
        cost_estimate=pl.CostEstimate(
            flops=6 * slots * fe * fq, bytes_accessed=12_000_000, transcendentals=slots * fe
        ),
    )(tok, down_weight[0], gate_weight[0], up_weight[0], gate_saved[0], up_saved[0])
    return out.reshape(NX, 2, tokens, fh).transpose(2, 0, 1, 3).reshape(tokens, width)


def solution(mesh):
    in_specs = (
        P(("dp", "expert", "etp"), None),
        P(("dp", "expert", "etp"), None),
        P(("dp", "expert", "etp"), None),
        P("expert", "etp", "dp"),
        P("expert", "dp", "etp"),
        P("expert", "dp", "etp"),
        P("expert", None, "etp"),
        P("expert", None, "etp"),
    )
    return jax.shard_map(
        on_device,
        mesh=mesh,
        in_specs=in_specs,
        out_specs=P(("dp", "expert", "etp"), None),
        check_vma=False,
    )
```

```python
import jax
import jax.numpy as jnp
from jax import lax
from jax.experimental import pallas as pl
from jax.experimental.pallas import tpu as pltpu
from jax.sharding import PartitionSpec as P

MESH = pl.DeviceIdType.MESH
NX, NZ, NT, NY = 4, 8, 8, 4
CAP = 6
ROWS = NX * CAP
META = 128
CHUNKS = (0, 1, -2, 3, 4, -3, 2, -1)
ORDER = (
    ("d1", 0), ("select", 0), ("z0", 0), ("gr", 0), ("gl", 0), ("select", 7), ("zf", -1),
    ("zf", 1), ("select", 1), ("ga", 0), ("hidden", 0), ("gr", 7), ("gl", 7), ("zf", -2),
    ("zf", 2), ("select", 2), ("select", 6), ("ga", 7), ("rb", 0), ("ra", 0), ("gl", 1),
    ("gr", 1), ("hidden", 7), ("ga", 1), ("select", 5), ("zf", 3), ("select", 3), ("rl", 0),
    ("gr", 2), ("gl", 2), ("hidden", 1), ("rb", 7), ("ra", 7), ("ga", 2), ("gl", 6), ("gr", 6),
    ("hidden", 2), ("select", 4), ("ga", 6), ("rb", 1), ("ra", 1), ("sb", 0), ("sa", 0),
    ("gl", 5), ("gr", 5), ("rl", 7), ("hidden", 6), ("rb", 2), ("ra", 2), ("ga", 5), ("rl", 1),
    ("gl", 3), ("gr", 3), ("hidden", 5), ("back", 0), ("ga", 3), ("rb", 6), ("gr", 4), ("ra", 6),
    ("gl", 4), ("rl", 2), ("sb", 7), ("sa", 7), ("ga", 4), ("sa", 1), ("sb", 1), ("sp", 0),
    ("rb", 5), ("ra", 5), ("hidden", 3), ("hidden", 4), ("rl", 6), ("sb", 2), ("sa", 2),
    ("back", 7), ("rl", 5), ("rb", 3), ("sl", 0), ("ra", 3), ("back", 1), ("rb", 4), ("sp", 7),
    ("ra", 4), ("sa", 6), ("sb", 6), ("back", 2), ("rl", 3), ("sp", 1), ("sb", 5), ("sa", 5),
    ("rl", 4), ("back", 6), ("sp", 2), ("sl", 7), ("sb", 3), ("sa", 3), ("back", 5), ("sp", 6),
    ("sl", 1), ("sb", 4), ("back", 3), ("sp", 5), ("sl", 2), ("sa", 4), ("sp", 3), ("sl", 6),
    ("back", 4), ("sl", 5), ("sp", 4), ("sl", 3), ("sl", 4), ("end", 0), ("fin", 0),
)
F32, BF16 = jnp.float32, jnp.bfloat16


def dot_nt(a, b):
    return lax.dot_general(a, b, (((1,), (1,)), ((), ())), preferred_element_type=F32)


def aligned(start, unit):
    return pl.multiple_of(start * unit, unit)


def kernel(
    tok, dw_hbm, gw_hbm, uw_hbm, gs_hbm, us_hbm, out,
    dw, gw, uw, gs, us, t2, rows, lhs, hp32, hp, xo, xl, xr, hf, gg, ug, sg, yb, pb, yr, zs, zr, fin, fr,
    load_sem, send_sem, recv_sem,
):
    d, e, t = lax.axis_index("dp"), lax.axis_index("expert"), lax.axis_index("etp")
    y, c = lax.div(t, 2), lax.rem(t, 2)
    fh = tok.shape[1] - META
    fq = 2 * fh
    fe = dw.shape[0]

    loads = []
    for i, (src, dst) in enumerate(
        ((dw_hbm, dw), (gs_hbm, gs), (us_hbm, us), (gw_hbm, gw), (uw_hbm, uw))
    ):
        loads.append(pltpu.make_async_copy(src, dst, load_sem.at[i]))
        loads[-1].start()

    def at_x(j):
        return (lax.rem(d + j + NX, NX), e, t)

    def at_y(j):
        return (d, e, 2 * lax.rem(y + j + NY, NY) + c)

    def at_z(j):
        return (d, lax.rem(e + j + NZ, NZ), t)

    sibling = (d, e, 2 * y + 1 - c)

    barrier = pltpu.get_barrier_semaphore()
    partners = [at_x(j) for j in range(1, NX)] + [at_z(j) for j in range(1, NZ)]
    partners += [at_y(j) for j in range(1, NY)] + [sibling]
    for device in partners:
        pl.semaphore_signal(barrier, inc=1, device_id=device, device_id_type=MESH)
    pl.semaphore_wait(barrier, len(partners))

    sent = []

    def send(src, dst, device):
        i = len(sent)
        copy = pltpu.make_async_remote_copy(
            src_ref=src,
            dst_ref=dst,
            send_sem=send_sem.at[i],
            recv_sem=recv_sem.at[i],
            device_id=device,
            device_id_type=MESH,
        )
        copy.start()
        sent.append(copy)
        return copy

    here = pl.ds(aligned(d, 16), 16)
    first, gather, returns, last = [], {}, [], []
    state = [dict() for _ in CHUNKS]
    seen = []

    def arrived(copy):
        if not any(copy is other for other in seen):
            seen.append(copy)
            copy.wait_recv()

    def d1(_):
        for j in range(1, NX):
            there = pl.ds(aligned(lax.rem(d + j, NX), 16), 16)
            first.append(send(tok.at[there, :], t2.at[0, here, :], at_x(j)))
        t2[0, here, :] = tok[here, :]

    def z0(_):
        for copy in first:
            arrived(copy)
        gather[1] = send(t2.at[0], t2.at[1], at_z(-1))
        gather[-1] = send(t2.at[0], t2.at[NZ - 1], at_z(1))

    def zf(r):
        arrived(gather[r])
        if r > 0:
            gather[r + 1] = send(t2.at[r], t2.at[r + 1], at_z(-1))
        else:
            gather[r - 1] = send(t2.at[NZ + r], t2.at[NZ + r - 1], at_z(1))

    def meta_of(r):
        return sum(
            t2[r % NZ, g * 16 : (g + 1) * 16, fh : fh + META].astype(F32) for g in range(NX)
        )

    def meta_row(meta, row):
        ids = lax.broadcasted_iota(jnp.int32, meta.shape, 0)
        return jnp.sum(jnp.where(ids == row, meta, 0.0), axis=0, keepdims=True)[:, :64]

    slot = lax.broadcasted_iota(jnp.int32, (ROWS, 64), 0)
    lane = lax.broadcasted_iota(jnp.int32, (ROWS, 64), 1)
    group = (
        (slot >= CAP).astype(jnp.int32)
        + (slot >= 2 * CAP).astype(jnp.int32)
        + (slot >= 3 * CAP).astype(jnp.int32)
    )
    place = (slot - CAP * group + 1).astype(F32)
    same_group = (lane >> 4) == group
    half_of_lane = (lane >> 3) & 1

    def choose(code, h):
        return same_group & (half_of_lane == h) & (code == place)

    t_left = 2 * lax.rem(y + NY - 1, NY) + c
    t_right = 2 * lax.rem(y + 1, NY) + c
    t_far = 2 * lax.rem(y + 2, NY) + c

    def select(k):
        r = CHUNKS[k]
        for copy in first if r == 0 else (gather[r],):
            arrived(copy)
        code = meta_row(meta_of(r), e)
        for h in range(2):
            part = jnp.dot(
                choose(code, h).astype(F32).astype(BF16),
                t2[r % NZ, :, 0:fh],
                preferred_element_type=F32,
            )
            rows[k, t, :, h * fh : (h + 1) * fh] = part.astype(BF16)
        block = rows.at[k, t]
        state[k]["ag"] = [send(block, block, device) for device in (at_y(1), at_y(-1), at_y(2))]
        state[k]["sib"] = [send(block, block, sibling)]

    def pass_on(k, i, there):
        state[k]["ag"][i].wait_recv()
        block = rows.at[k, there]
        state[k]["sib"].append(send(block, block, sibling))

    def gl(k):
        pass_on(k, 0, t_left)

    def gr(k):
        pass_on(k, 1, t_right)

    def ga(k):
        pass_on(k, 2, t_far)

    q_right, q_left = lax.rem(d + 1, NX), lax.rem(d + NX - 1, NX)
    q_far = lax.rem(d + 2, NX)
    half_a, half_b = slice(0, fe // 2), slice(fe // 2, fe)

    def quarter(q):
        return pl.ds(aligned(q, 2 * ROWS), 2 * ROWS)

    def hidden(k):
        for copy in state[k]["sib"]:
            copy.wait_recv()
        if loads[0] is not None:
            loads[0].wait()
            loads[0] = None
        lhs[...] = rows[k].astype(F32).reshape(NT * ROWS, fq).astype(BF16)
        tile = min(256, fe)

        @pl.loop(0, fe // tile)
        def _(n):
            cols = pl.ds(pl.multiple_of(n * tile, tile), tile)
            part = dot_nt(lhs[...], dw[cols, :])
            hp32[k, :, cols] = part
            hp[k, :, cols] = part.astype(BF16)

        far, right, left = quarter(q_far), quarter(q_right), quarter(q_left)
        far_a = send(hp.at[k, far, half_a], xo.at[k, :, half_a], at_x(1))
        far_b = send(hp.at[k, far, half_b], xo.at[k, :, half_b], at_x(-1))
        near_b = send(hp.at[k, right, half_b], xl.at[k, :, half_b], at_x(1))
        near_a = send(hp.at[k, left, half_a], xr.at[k, :, half_a], at_x(-1))
        state[k]["rs"] = (far_a, far_b)
        state[k]["rs2"] = [near_b, near_a]

    def add_far(k, i, to, half, dst, device):
        state[k]["rs"][i].wait_recv()
        hp[k, to, half] = (hp32[k, to, half] + xo[k, :, half].astype(F32)).astype(BF16)
        state[k]["rs2"].append(send(hp.at[k, to, half], dst.at[k, :, half], device))

    def ra(k):
        add_far(k, 0, quarter(q_right), half_a, xl, at_x(1))

    def rb(k):
        add_far(k, 1, quarter(q_left), half_b, xr, at_x(-1))

    def rl(k):
        for copy in state[k]["rs2"]:
            copy.wait_recv()
        mine = quarter(d)
        total = hp32[k, mine, :] + xl[k].astype(F32) + xr[k].astype(F32)
        hf[k, mine, :] = total.astype(BF16)
        block = hf.at[k, mine, :]
        state[k]["hg"] = (send(block, block, at_x(1)), send(block, block, at_x(-1)))
        state[k]["hg2"] = []

    def sa(k):
        state[k]["hg"][0].wait_recv()
        block = hf.at[k, quarter(q_left), half_a]
        state[k]["hg2"].append(send(block, block, at_x(1)))

    def sb(k):
        state[k]["hg"][1].wait_recv()
        block = hf.at[k, quarter(q_right), half_b]
        state[k]["hg2"].append(send(block, block, at_x(-1)))

    def back(k):
        for copy in state[k]["hg2"]:
            copy.wait_recv()
        while len(loads) > 1:
            loads.pop().wait()
        source = lax.rem(e + CHUNKS[k] + NZ, NZ)
        slots = pl.ds(aligned(source, NT * ROWS), NT * ROWS)

        @pl.loop(0, fe // 128)
        def _(n):
            cols = pl.ds(pl.multiple_of(n * 128, 128), 128)
            h = hf[k, :, cols].astype(F32)
            gate = gs[slots, cols].astype(F32)
            up = us[slots, cols].astype(F32)
            s = jax.nn.sigmoid(gate)
            gg[:, cols] = (h * up * s * (1.0 + gate * (1.0 - s))).astype(BF16)
            ug[:, cols] = (h * gate * s).astype(BF16)

        tile = 512 if fq % 512 == 0 else min(256, fq)

        @pl.loop(0, fq // tile)
        def _(n):
            cols = pl.ds(pl.multiple_of(n * tile, tile), tile)
            part = dot_nt(gg[...], gw[cols, :]) + dot_nt(ug[...], uw[cols, :])
            for i in range(NT):
                sg[k, i // 2, i % 2, :, cols] = part[i * ROWS : (i + 1) * ROWS]

        state[k]["pair"] = send(sg.at[k, :, 1 - c], yb.at[k], sibling)

    def sp(k):
        state[k]["pair"].wait_recv()
        state[k]["ys"] = []
        for i in range(1, NY):
            q = lax.rem(y + i, NY)
            pb[k, i - 1] = (sg[k, q, c] + yb[k, q]).astype(BF16)
            state[k]["ys"].append(send(pb.at[k, i - 1], yr.at[k, i - 1], at_y(i)))

    def sl(k):
        for copy in state[k]["ys"]:
            copy.wait_recv()
        total = sg[k, y, c] + yb[k, y]
        for i in range(NY - 1):
            total = total + yr[k, i].astype(F32)
        r = CHUNKS[k]
        if r == 0:
            zr[0] = total
        else:
            zs[k] = total
            returns.append(send(zs.at[k], zr.at[(-r) % NZ], at_z(r)))

    def end(_):
        meta = meta_of(0)
        mix = [[], []]
        for j in range(NZ):
            x = lax.rem(e + j, NZ)
            code, weight = meta_row(meta, x), meta_row(meta, x + NZ)
            for h in range(2):
                mix[h].append(jnp.where(choose(code, h), weight, 0.0))
        mix = [jnp.concatenate(m, axis=0).astype(BF16) for m in mix]
        for copy in returns:
            copy.wait_recv()

        def combine(h):
            value = zr[:, :, h * fh : (h + 1) * fh].reshape(NZ * ROWS, fh)
            coarse = value.astype(BF16)
            fine = (value - coarse.astype(F32)).astype(BF16)
            dims = (((0,), (0,)), ((), ()))
            return lax.dot_general(mix[h], coarse, dims, preferred_element_type=F32) + lax.dot_general(
                mix[h], fine, dims, preferred_element_type=F32
            )

        fin[...] = (combine(0) + combine(1)).astype(BF16)
        for j in range(1, NX):
            there = pl.ds(aligned(lax.rem(d + j, NX), 16), 16)
            last.append(send(fin.at[there, :], fr.at[here, :], at_x(j)))
        fr[here, :] = fin[here, :]

    def finish(_):
        for copy in last:
            copy.wait_recv()
        out[...] = fr[...]

    stages = {
        "d1": d1, "z0": z0, "zf": zf, "select": select, "gl": gl, "gr": gr, "ga": ga,
        "hidden": hidden, "ra": ra, "rb": rb, "rl": rl, "sa": sa, "sb": sb,
        "back": back, "sp": sp, "sl": sl, "end": end, "fin": finish,
    }
    for name, k in ORDER:
        stages[name](k)
    for copy in sent:
        copy.wait_send()


COPIES = 3 + 7 + 8 * (4 + 3 + 4 + 2 + 2 + 2 + 1 + 3) + 7 + 3


def on_device(
    grad_output, comb_weights, expert_ids, down_weight, gate_weight, up_weight, gate_saved, up_saved
):
    tokens, width = grad_output.shape
    fq = width // NX
    fh = fq // 2
    fe = down_weight.shape[1]
    slots = gate_saved.shape[1]
    d = lax.axis_index("dp")
    experts = jnp.arange(NZ, dtype=jnp.int32)
    match = expert_ids[None, :, :] == experts[:, None, None]
    hits = jnp.any(match, axis=2)
    earlier = jnp.arange(tokens)[:, None] < jnp.arange(tokens)[None, :]
    before = jnp.sum(jnp.where(hits[:, :, None] & earlier[None], 1.0, 0.0), axis=1)
    code = jnp.where(hits, before + 1.0, 0.0)
    weight = jnp.sum(jnp.where(match, comb_weights.astype(F32)[None], 0.0), axis=2)
    meta = jnp.concatenate([code, weight], axis=0).astype(BF16)
    lanes = jnp.arange(META) // 16 == d
    meta = jnp.where(lanes[None, :], jnp.tile(meta, (1, META // tokens)), 0)
    value = grad_output.reshape(tokens, NX, 2, fh).transpose(1, 2, 0, 3).reshape(NX, 16, fh)
    tok = jnp.concatenate([value, jnp.broadcast_to(meta[None], (NX, 16, META))], axis=2)
    tok = tok.reshape(NX * 16, fh + META)

    n = len(CHUNKS)
    vmem = pltpu.VMEM
    any_space = pl.BlockSpec(memory_space=pl.ANY)
    in_vmem = pl.BlockSpec(memory_space=pltpu.VMEM)
    out = pl.pallas_call(
        kernel,
        out_shape=jax.ShapeDtypeStruct((NX * 16, fh), BF16),
        in_specs=[in_vmem] + [any_space] * 5,
        out_specs=in_vmem,
        scratch_shapes=[
            vmem((fe, fq), BF16),
            vmem((fq, fe), BF16),
            vmem((fq, fe), BF16),
            vmem((slots, fe), BF16),
            vmem((slots, fe), BF16),
            vmem((NZ, 64, fh + META), BF16),
            vmem((n, NT, ROWS, fq), BF16),
            vmem((NT * ROWS, fq), BF16),
            vmem((n, NT * ROWS, fe), F32),
            vmem((n, NT * ROWS, fe), BF16),
            vmem((n, 2 * ROWS, fe), BF16),
            vmem((n, 2 * ROWS, fe), BF16),
            vmem((n, 2 * ROWS, fe), BF16),
            vmem((n, NT * ROWS, fe), BF16),
            vmem((NT * ROWS, fe), BF16),
            vmem((NT * ROWS, fe), BF16),
            vmem((n, NY, 2, ROWS, fq), F32),
            vmem((n, NY, ROWS, fq), F32),
            vmem((n, NY - 1, ROWS, fq), BF16),
            vmem((n, NY - 1, ROWS, fq), BF16),
            vmem((n, ROWS, fq), F32),
            vmem((NZ, ROWS, fq), F32),
            vmem((64, fh), BF16),
            vmem((64, fh), BF16),
            pltpu.SemaphoreType.DMA((5,)),
            pltpu.SemaphoreType.DMA((COPIES,)),
            pltpu.SemaphoreType.DMA((COPIES,)),
        ],
        compiler_params=pltpu.CompilerParams(
            collective_id=0, has_side_effects=True, vmem_limit_bytes=58 * 1024 * 1024
        ),
        cost_estimate=pl.CostEstimate(
            flops=6 * slots * fe * fq, bytes_accessed=12_000_000, transcendentals=slots * fe
        ),
    )(tok, down_weight[0], gate_weight[0], up_weight[0], gate_saved[0], up_saved[0])
    return out.reshape(NX, 2, tokens, fh).transpose(2, 0, 1, 3).reshape(tokens, width)


def solution(mesh):
    in_specs = (
        P(("dp", "expert", "etp"), None),
        P(("dp", "expert", "etp"), None),
        P(("dp", "expert", "etp"), None),
        P("expert", "etp", "dp"),
        P("expert", "dp", "etp"),
        P("expert", "dp", "etp"),
        P("expert", None, "etp"),
        P("expert", None, "etp"),
    )
    return jax.shard_map(
        on_device,
        mesh=mesh,
        in_specs=in_specs,
        out_specs=P(("dp", "expert", "etp"), None),
        check_vma=False,
    )
```

```python
import jax
import jax.numpy as jnp
from jax import lax
from jax.experimental import pallas as pl
from jax.experimental.pallas import tpu as pltpu
from jax.sharding import PartitionSpec as P

MESH = pl.DeviceIdType.MESH
NX, NZ, NT, NY = 4, 8, 8, 4
CAP = 6
ROWS = NX * CAP
META = 128
CHUNKS = (0, 1, -2, 3, 4, -3, 2, -1)
ORDER = (
    ("d1", 0), ("select", 0), ("z0", 0), ("gr", 0), ("gl", 0), ("select", 7), ("zf", -1),
    ("zf", 1), ("select", 1), ("ga", 0), ("hidden", 0), ("gr", 7), ("gl", 7), ("zf", -2),
    ("zf", 2), ("select", 2), ("select", 6), ("ga", 7), ("rb", 0), ("ra", 0), ("gl", 1),
    ("gr", 1), ("hidden", 7), ("ga", 1), ("select", 5), ("zf", 3), ("select", 3), ("rl", 0),
    ("gr", 2), ("gl", 2), ("hidden", 1), ("rb", 7), ("ra", 7), ("ga", 2), ("gl", 6), ("gr", 6),
    ("hidden", 2), ("select", 4), ("ga", 6), ("rb", 1), ("ra", 1), ("sb", 0), ("sa", 0),
    ("gl", 5), ("gr", 5), ("rl", 7), ("hidden", 6), ("rb", 2), ("ra", 2), ("ga", 5), ("rl", 1),
    ("gl", 3), ("gr", 3), ("hidden", 5), ("back", 0), ("ga", 3), ("rb", 6), ("gr", 4), ("ra", 6),
    ("gl", 4), ("rl", 2), ("sb", 7), ("sa", 7), ("ga", 4), ("sa", 1), ("sb", 1), ("sp", 0),
    ("rb", 5), ("ra", 5), ("hidden", 3), ("hidden", 4), ("rl", 6), ("sb", 2), ("sa", 2),
    ("back", 7), ("rl", 5), ("rb", 3), ("sl", 0), ("ra", 3), ("back", 1), ("rb", 4), ("sp", 7),
    ("ra", 4), ("sa", 6), ("sb", 6), ("back", 2), ("rl", 3), ("sp", 1), ("sb", 5), ("sa", 5),
    ("rl", 4), ("back", 6), ("sp", 2), ("sl", 7), ("sb", 3), ("sa", 3), ("back", 5), ("sp", 6),
    ("sl", 1), ("sb", 4), ("back", 3), ("sp", 5), ("sl", 2), ("sa", 4), ("sp", 3), ("sl", 6),
    ("back", 4), ("sl", 5), ("sp", 4), ("sl", 3), ("sl", 4), ("end", 0), ("fin", 0),
)
F32, BF16 = jnp.float32, jnp.bfloat16


def dot_nt(a, b):
    return lax.dot_general(a, b, (((1,), (1,)), ((), ())), preferred_element_type=F32)


def aligned(start, unit):
    return pl.multiple_of(start * unit, unit)


def kernel(
    grad, ids, comb, dw_hbm, gw_hbm, uw_hbm, gs_hbm, us_hbm, out,
    dw, gw, uw, gs, us, tok, t2, rows, lhs, hp32, hp, xo, xl, xr, hf, gg, ug, sg, yb, pb, yr, zs, zr, fin, fr,
    load_sem, send_sem, recv_sem,
):
    d, e, t = lax.axis_index("dp"), lax.axis_index("expert"), lax.axis_index("etp")
    y, c = lax.div(t, 2), lax.rem(t, 2)
    fq = grad.shape[1] // NX
    fh = fq // 2
    fe = dw.shape[0]

    loads = []
    for i, (src, dst) in enumerate(
        ((dw_hbm, dw), (gs_hbm, gs), (us_hbm, us), (gw_hbm, gw), (uw_hbm, uw))
    ):
        loads.append(pltpu.make_async_copy(src, dst, load_sem.at[i]))
        loads[-1].start()

    def at_x(j):
        return (lax.rem(d + j + NX, NX), e, t)

    def at_y(j):
        return (d, e, 2 * lax.rem(y + j + NY, NY) + c)

    def at_z(j):
        return (d, lax.rem(e + j + NZ, NZ), t)

    sibling = (d, e, 2 * y + 1 - c)

    barrier = pltpu.get_barrier_semaphore()
    partners = [at_x(j) for j in range(1, NX)] + [at_z(j) for j in range(1, NZ)]
    partners += [at_y(j) for j in range(1, NY)] + [sibling]
    for device in partners:
        pl.semaphore_signal(barrier, inc=1, device_id=device, device_id_type=MESH)

    tokens = grad.shape[0]
    experts = lax.broadcasted_iota(jnp.int32, (NZ, tokens), 0)
    choices = [ids[i : i + 1, :] == experts for i in range(ids.shape[0])]
    hits = sum(jnp.where(m, 1.0, 0.0) for m in choices)
    weight = sum(
        jnp.where(m, comb[i : i + 1, :].astype(F32), 0.0) for i, m in enumerate(choices)
    )
    earlier = lax.broadcasted_iota(jnp.int32, (tokens, tokens), 0) < lax.broadcasted_iota(
        jnp.int32, (tokens, tokens), 1
    )
    before = jnp.dot(
        hits.astype(BF16), jnp.where(earlier, 1.0, 0.0).astype(BF16), preferred_element_type=F32
    )
    code = jnp.where(hits > 0.0, before + 1.0, 0.0)
    lanes = lax.broadcasted_iota(jnp.int32, (tokens, META), 1)
    token = lax.broadcasted_iota(jnp.int32, (tokens, META), 0)
    spread = jnp.where(((lanes >> 4) == d) & ((lanes & 7) == token), 1.0, 0.0).astype(BF16)
    meta_here = jnp.dot(
        jnp.concatenate([code, weight], axis=0).astype(BF16), spread, preferred_element_type=F32
    ).astype(BF16)
    for q in range(NX):
        parts = [grad[:, (2 * q + h) * fh : (2 * q + h + 1) * fh].astype(F32) for h in range(2)]
        tok[q * 16 : (q + 1) * 16, 0:fh] = jnp.concatenate(parts, axis=0).astype(BF16)
        tok[q * 16 : (q + 1) * 16, fh : fh + META] = meta_here
    pl.semaphore_wait(barrier, len(partners))

    sent = []

    def send(src, dst, device):
        i = len(sent)
        copy = pltpu.make_async_remote_copy(
            src_ref=src,
            dst_ref=dst,
            send_sem=send_sem.at[i],
            recv_sem=recv_sem.at[i],
            device_id=device,
            device_id_type=MESH,
        )
        copy.start()
        sent.append(copy)
        return copy

    here = pl.ds(aligned(d, 16), 16)
    first, gather, returns, last = [], {}, [], []
    state = [dict() for _ in CHUNKS]
    seen = []

    def arrived(copy):
        if not any(copy is other for other in seen):
            seen.append(copy)
            copy.wait_recv()

    def d1(_):
        for j in range(1, NX):
            there = pl.ds(aligned(lax.rem(d + j, NX), 16), 16)
            first.append(send(tok.at[there, :], t2.at[0, here, :], at_x(j)))
        t2[0, here, :] = tok[here, :]

    def z0(_):
        for copy in first:
            arrived(copy)
        gather[1] = send(t2.at[0], t2.at[1], at_z(-1))
        gather[-1] = send(t2.at[0], t2.at[NZ - 1], at_z(1))

    def zf(r):
        arrived(gather[r])
        if r > 0:
            gather[r + 1] = send(t2.at[r], t2.at[r + 1], at_z(-1))
        else:
            gather[r - 1] = send(t2.at[NZ + r], t2.at[NZ + r - 1], at_z(1))

    def meta_of(r):
        return sum(
            t2[r % NZ, g * 16 : (g + 1) * 16, fh : fh + META].astype(F32) for g in range(NX)
        )

    def meta_row(meta, row):
        ids = lax.broadcasted_iota(jnp.int32, meta.shape, 0)
        return jnp.sum(jnp.where(ids == row, meta, 0.0), axis=0, keepdims=True)[:, :64]

    slot = lax.broadcasted_iota(jnp.int32, (ROWS, 64), 0)
    lane = lax.broadcasted_iota(jnp.int32, (ROWS, 64), 1)
    group = (
        (slot >= CAP).astype(jnp.int32)
        + (slot >= 2 * CAP).astype(jnp.int32)
        + (slot >= 3 * CAP).astype(jnp.int32)
    )
    place = (slot - CAP * group + 1).astype(F32)
    same_group = (lane >> 4) == group
    half_of_lane = (lane >> 3) & 1

    def choose(code, h):
        return same_group & (half_of_lane == h) & (code == place)

    t_left = 2 * lax.rem(y + NY - 1, NY) + c
    t_right = 2 * lax.rem(y + 1, NY) + c
    t_far = 2 * lax.rem(y + 2, NY) + c

    def select(k):
        r = CHUNKS[k]
        for copy in first if r == 0 else (gather[r],):
            arrived(copy)
        code = meta_row(meta_of(r), e)
        for h in range(2):
            part = jnp.dot(
                choose(code, h).astype(F32).astype(BF16),
                t2[r % NZ, :, 0:fh],
                preferred_element_type=F32,
            )
            rows[k, t, :, h * fh : (h + 1) * fh] = part.astype(BF16)
        block = rows.at[k, t]
        state[k]["ag"] = [send(block, block, device) for device in (at_y(1), at_y(-1), at_y(2))]
        state[k]["sib"] = [send(block, block, sibling)]

    def pass_on(k, i, there):
        state[k]["ag"][i].wait_recv()
        block = rows.at[k, there]
        state[k]["sib"].append(send(block, block, sibling))

    def gl(k):
        pass_on(k, 0, t_left)

    def gr(k):
        pass_on(k, 1, t_right)

    def ga(k):
        pass_on(k, 2, t_far)

    q_right, q_left = lax.rem(d + 1, NX), lax.rem(d + NX - 1, NX)
    q_far = lax.rem(d + 2, NX)
    half_a, half_b = slice(0, fe // 2), slice(fe // 2, fe)

    def quarter(q):
        return pl.ds(aligned(q, 2 * ROWS), 2 * ROWS)

    def hidden(k):
        for copy in state[k]["sib"]:
            copy.wait_recv()
        if loads[0] is not None:
            loads[0].wait()
            loads[0] = None
        lhs[...] = rows[k].astype(F32).reshape(NT * ROWS, fq).astype(BF16)
        tile = min(256, fe)

        @pl.loop(0, fe // tile)
        def _(n):
            cols = pl.ds(pl.multiple_of(n * tile, tile), tile)
            part = dot_nt(lhs[...], dw[cols, :])
            hp32[k, :, cols] = part
            hp[k, :, cols] = part.astype(BF16)

        far, right, left = quarter(q_far), quarter(q_right), quarter(q_left)
        far_a = send(hp.at[k, far, half_a], xo.at[k, :, half_a], at_x(1))
        far_b = send(hp.at[k, far, half_b], xo.at[k, :, half_b], at_x(-1))
        near_b = send(hp.at[k, right, half_b], xl.at[k, :, half_b], at_x(1))
        near_a = send(hp.at[k, left, half_a], xr.at[k, :, half_a], at_x(-1))
        state[k]["rs"] = (far_a, far_b)
        state[k]["rs2"] = [near_b, near_a]

    def add_far(k, i, to, half, dst, device):
        state[k]["rs"][i].wait_recv()
        hp[k, to, half] = (hp32[k, to, half] + xo[k, :, half].astype(F32)).astype(BF16)
        state[k]["rs2"].append(send(hp.at[k, to, half], dst.at[k, :, half], device))

    def ra(k):
        add_far(k, 0, quarter(q_right), half_a, xl, at_x(1))

    def rb(k):
        add_far(k, 1, quarter(q_left), half_b, xr, at_x(-1))

    def rl(k):
        for copy in state[k]["rs2"]:
            copy.wait_recv()
        mine = quarter(d)
        total = hp32[k, mine, :] + xl[k].astype(F32) + xr[k].astype(F32)
        hf[k, mine, :] = total.astype(BF16)
        block = hf.at[k, mine, :]
        state[k]["hg"] = (send(block, block, at_x(1)), send(block, block, at_x(-1)))
        state[k]["hg2"] = []

    def sa(k):
        state[k]["hg"][0].wait_recv()
        block = hf.at[k, quarter(q_left), half_a]
        state[k]["hg2"].append(send(block, block, at_x(1)))

    def sb(k):
        state[k]["hg"][1].wait_recv()
        block = hf.at[k, quarter(q_right), half_b]
        state[k]["hg2"].append(send(block, block, at_x(-1)))

    def back(k):
        for copy in state[k]["hg2"]:
            copy.wait_recv()
        while len(loads) > 1:
            loads.pop().wait()
        source = lax.rem(e + CHUNKS[k] + NZ, NZ)
        slots = pl.ds(aligned(source, NT * ROWS), NT * ROWS)

        @pl.loop(0, fe // 128)
        def _(n):
            cols = pl.ds(pl.multiple_of(n * 128, 128), 128)
            h = hf[k, :, cols].astype(F32)
            gate = gs[slots, cols].astype(F32)
            up = us[slots, cols].astype(F32)
            s = jax.nn.sigmoid(gate)
            gg[:, cols] = (h * up * s * (1.0 + gate * (1.0 - s))).astype(BF16)
            ug[:, cols] = (h * gate * s).astype(BF16)

        tile = 512 if fq % 512 == 0 else min(256, fq)

        @pl.loop(0, fq // tile)
        def _(n):
            cols = pl.ds(pl.multiple_of(n * tile, tile), tile)
            part = dot_nt(gg[...], gw[cols, :]) + dot_nt(ug[...], uw[cols, :])
            for i in range(NT):
                sg[k, i // 2, i % 2, :, cols] = part[i * ROWS : (i + 1) * ROWS]

        state[k]["pair"] = send(sg.at[k, :, 1 - c], yb.at[k], sibling)

    def sp(k):
        state[k]["pair"].wait_recv()
        state[k]["ys"] = []
        for i in range(1, NY):
            q = lax.rem(y + i, NY)
            pb[k, i - 1] = (sg[k, q, c] + yb[k, q]).astype(BF16)
            state[k]["ys"].append(send(pb.at[k, i - 1], yr.at[k, i - 1], at_y(i)))

    def sl(k):
        for copy in state[k]["ys"]:
            copy.wait_recv()
        total = sg[k, y, c] + yb[k, y]
        for i in range(NY - 1):
            total = total + yr[k, i].astype(F32)
        r = CHUNKS[k]
        if r == 0:
            zr[0] = total
        else:
            zs[k] = total
            returns.append(send(zs.at[k], zr.at[(-r) % NZ], at_z(r)))

    def end(_):
        meta = meta_of(0)
        mix = [[], []]
        for j in range(NZ):
            x = lax.rem(e + j, NZ)
            code, weight = meta_row(meta, x), meta_row(meta, x + NZ)
            for h in range(2):
                mix[h].append(jnp.where(choose(code, h), weight, 0.0))
        mix = [jnp.concatenate(m, axis=0).astype(BF16) for m in mix]
        for copy in returns:
            copy.wait_recv()

        def combine(h):
            value = zr[:, :, h * fh : (h + 1) * fh].reshape(NZ * ROWS, fh)
            coarse = value.astype(BF16)
            fine = (value - coarse.astype(F32)).astype(BF16)
            dims = (((0,), (0,)), ((), ()))
            return lax.dot_general(mix[h], coarse, dims, preferred_element_type=F32) + lax.dot_general(
                mix[h], fine, dims, preferred_element_type=F32
            )

        fin[...] = (combine(0) + combine(1)).astype(BF16)
        for j in range(1, NX):
            there = pl.ds(aligned(lax.rem(d + j, NX), 16), 16)
            last.append(send(fin.at[there, :], fr.at[here, :], at_x(j)))
        fr[here, :] = fin[here, :]

    def finish(_):
        for copy in last:
            copy.wait_recv()
        for q in range(NX):
            both = fr[q * 16 : (q + 1) * 16, :].astype(F32)
            for h in range(2):
                cols = slice((2 * q + h) * fh, (2 * q + h + 1) * fh)
                out[:, cols] = both[h * tokens : (h + 1) * tokens].astype(BF16)

    stages = {
        "d1": d1, "z0": z0, "zf": zf, "select": select, "gl": gl, "gr": gr, "ga": ga,
        "hidden": hidden, "ra": ra, "rb": rb, "rl": rl, "sa": sa, "sb": sb,
        "back": back, "sp": sp, "sl": sl, "end": end, "fin": finish,
    }
    for name, k in ORDER:
        stages[name](k)
    for copy in sent:
        copy.wait_send()


COPIES = 3 + 7 + 8 * (4 + 3 + 4 + 2 + 2 + 2 + 1 + 3) + 7 + 3


def on_device(
    grad_output, comb_weights, expert_ids, down_weight, gate_weight, up_weight, gate_saved, up_saved
):
    tokens, width = grad_output.shape
    fq = width // NX
    fh = fq // 2
    fe = down_weight.shape[1]
    slots = gate_saved.shape[1]
    n = len(CHUNKS)
    vmem = pltpu.VMEM
    any_space = pl.BlockSpec(memory_space=pl.ANY)
    in_vmem = pl.BlockSpec(memory_space=pltpu.VMEM)
    return pl.pallas_call(
        kernel,
        out_shape=jax.ShapeDtypeStruct((tokens, width), BF16),
        in_specs=[in_vmem] * 3 + [any_space] * 5,
        out_specs=in_vmem,
        scratch_shapes=[
            vmem((fe, fq), BF16),
            vmem((fq, fe), BF16),
            vmem((fq, fe), BF16),
            vmem((slots, fe), BF16),
            vmem((slots, fe), BF16),
            vmem((NX * 16, fh + META), BF16),
            vmem((NZ, 64, fh + META), BF16),
            vmem((n, NT, ROWS, fq), BF16),
            vmem((NT * ROWS, fq), BF16),
            vmem((n, NT * ROWS, fe), F32),
            vmem((n, NT * ROWS, fe), BF16),
            vmem((n, 2 * ROWS, fe), BF16),
            vmem((n, 2 * ROWS, fe), BF16),
            vmem((n, 2 * ROWS, fe), BF16),
            vmem((n, NT * ROWS, fe), BF16),
            vmem((NT * ROWS, fe), BF16),
            vmem((NT * ROWS, fe), BF16),
            vmem((n, NY, 2, ROWS, fq), F32),
            vmem((n, NY, ROWS, fq), F32),
            vmem((n, NY - 1, ROWS, fq), BF16),
            vmem((n, NY - 1, ROWS, fq), BF16),
            vmem((n, ROWS, fq), F32),
            vmem((NZ, ROWS, fq), F32),
            vmem((64, fh), BF16),
            vmem((64, fh), BF16),
            pltpu.SemaphoreType.DMA((5,)),
            pltpu.SemaphoreType.DMA((COPIES,)),
            pltpu.SemaphoreType.DMA((COPIES,)),
        ],
        compiler_params=pltpu.CompilerParams(
            collective_id=0, has_side_effects=True, vmem_limit_bytes=58 * 1024 * 1024
        ),
        cost_estimate=pl.CostEstimate(
            flops=6 * slots * fe * fq, bytes_accessed=12_000_000, transcendentals=slots * fe
        ),
    )(
        grad_output, expert_ids.T, comb_weights.T,
        down_weight[0], gate_weight[0], up_weight[0], gate_saved[0], up_saved[0],
    )


def solution(mesh):
    in_specs = (
        P(("dp", "expert", "etp"), None),
        P(("dp", "expert", "etp"), None),
        P(("dp", "expert", "etp"), None),
        P("expert", "etp", "dp"),
        P("expert", "dp", "etp"),
        P("expert", "dp", "etp"),
        P("expert", None, "etp"),
        P("expert", None, "etp"),
    )
    return jax.shard_map(
        on_device,
        mesh=mesh,
        in_specs=in_specs,
        out_specs=P(("dp", "expert", "etp"), None),
        check_vma=False,
    )
```

```python
import jax
import jax.numpy as jnp
from jax import lax
from jax.experimental import pallas as pl
from jax.experimental.pallas import tpu as pltpu
from jax.sharding import PartitionSpec as P

MESH = pl.DeviceIdType.MESH
NX, NZ, NT, NY = 4, 8, 8, 4
CAP = 6
ROWS = NX * CAP
META = 128
FAR = 3
CHUNKS = (0, 1, -2, 3, 4, -3, 2, -1)
ORDER = (
    ("d1", 0), ("select", 0), ("z0", 0), ("gr", 0), ("gl", 0), ("zf", 1), ("zf", -1),
    ("select", 1), ("select", 7), ("ga", 0), ("hidden", 0), ("gr", 1), ("gl", 1), ("select", 6),
    ("zf", 2), ("zf", -2), ("select", 2), ("ga", 1), ("rb", 0), ("ra", 0), ("gr", 7), ("gl", 7),
    ("hidden", 1), ("ga", 7), ("zf", 3), ("select", 3), ("select", 5), ("gr", 6), ("gl", 6),
    ("rl", 0), ("hidden", 7), ("ra", 1), ("rb", 1), ("ga", 6), ("gl", 2), ("gr", 2),
    ("select", 4), ("sb", 0), ("sa", 0), ("hidden", 6), ("ra", 7), ("rb", 7), ("ga", 2),
    ("gl", 3), ("gr", 3), ("rl", 1), ("hidden", 2), ("ra", 6), ("rb", 6), ("back", 0), ("gr", 5),
    ("gl", 5), ("rl", 7), ("ga", 3), ("sb", 1), ("sa", 1), ("ga", 5), ("ra", 2), ("rb", 2),
    ("gl", 4), ("gr", 4), ("sp", 0), ("rl", 6), ("hidden", 3), ("ga", 4), ("hidden", 5),
    ("sb", 7), ("sa", 7), ("back", 1), ("sb", 6), ("rl", 2), ("sa", 6), ("ra", 3), ("rb", 3),
    ("hidden", 4), ("sl", 0), ("ra", 5), ("rb", 5), ("sp", 1), ("back", 7), ("sb", 2), ("sa", 2),
    ("back", 6), ("rl", 3), ("sp", 7), ("rl", 5), ("ra", 4), ("sl", 1), ("rb", 4), ("back", 2),
    ("sp", 6), ("sb", 3), ("sa", 3), ("sa", 5), ("sb", 5), ("rl", 4), ("sp", 2), ("sl", 7),
    ("back", 3), ("back", 5), ("sb", 4), ("sa", 4), ("sl", 6), ("sp", 3), ("sl", 2), ("sp", 5),
    ("back", 4), ("sl", 3), ("sp", 4), ("sl", 5), ("sl", 4), ("end", 0), ("fin", 0),
)
F32, BF16 = jnp.float32, jnp.bfloat16


def dot_nt(a, b):
    return lax.dot_general(a, b, (((1,), (1,)), ((), ())), preferred_element_type=F32)


def aligned(start, unit):
    return pl.multiple_of(start * unit, unit)


def kernel(
    grad, ids, comb, dw_hbm, gw_hbm, uw_hbm, gs_hbm, us_hbm, out,
    dw, gw, uw, gs, us, tok, t2, rows, lhs, hp32, hp, xo, xl, xr, hf, gg, ug, sg, yb, pb, yr, zs, zr, zs_far, zr_far, fin, fr,
    load_sem, send_sem, recv_sem,
):
    d, e, t = lax.axis_index("dp"), lax.axis_index("expert"), lax.axis_index("etp")
    y, c = lax.div(t, 2), lax.rem(t, 2)
    fq = grad.shape[1] // NX
    fh = fq // 2
    fe = dw.shape[0]

    loads = []
    for i, (src, dst) in enumerate(
        ((dw_hbm, dw), (gs_hbm, gs), (us_hbm, us), (gw_hbm, gw), (uw_hbm, uw))
    ):
        loads.append(pltpu.make_async_copy(src, dst, load_sem.at[i]))
        loads[-1].start()

    def at_x(j):
        return (lax.rem(d + j + NX, NX), e, t)

    def at_y(j):
        return (d, e, 2 * lax.rem(y + j + NY, NY) + c)

    def at_z(j):
        return (d, lax.rem(e + j + NZ, NZ), t)

    sibling = (d, e, 2 * y + 1 - c)

    barrier = pltpu.get_barrier_semaphore()
    partners = [at_x(j) for j in range(1, NX)] + [at_z(j) for j in range(1, NZ)]
    partners += [at_y(j) for j in range(1, NY)] + [sibling]
    for device in partners:
        pl.semaphore_signal(barrier, inc=1, device_id=device, device_id_type=MESH)

    tokens = grad.shape[0]
    experts = lax.broadcasted_iota(jnp.int32, (NZ, tokens), 0)
    choices = [ids[i : i + 1, :] == experts for i in range(ids.shape[0])]
    hits = sum(jnp.where(m, 1.0, 0.0) for m in choices)
    weight = sum(
        jnp.where(m, comb[i : i + 1, :].astype(F32), 0.0) for i, m in enumerate(choices)
    )
    earlier = lax.broadcasted_iota(jnp.int32, (tokens, tokens), 0) < lax.broadcasted_iota(
        jnp.int32, (tokens, tokens), 1
    )
    before = jnp.dot(
        hits.astype(BF16), jnp.where(earlier, 1.0, 0.0).astype(BF16), preferred_element_type=F32
    )
    code = jnp.where(hits > 0.0, before + 1.0, 0.0)
    lanes = lax.broadcasted_iota(jnp.int32, (tokens, META), 1)
    token = lax.broadcasted_iota(jnp.int32, (tokens, META), 0)
    spread = jnp.where(((lanes >> 4) == d) & ((lanes & 7) == token), 1.0, 0.0).astype(BF16)
    meta_here = jnp.dot(
        jnp.concatenate([code, weight], axis=0).astype(BF16), spread, preferred_element_type=F32
    ).astype(BF16)
    for q in range(NX):
        parts = [grad[:, (2 * q + h) * fh : (2 * q + h + 1) * fh].astype(F32) for h in range(2)]
        tok[q * 16 : (q + 1) * 16, 0:fh] = jnp.concatenate(parts, axis=0).astype(BF16)
        tok[q * 16 : (q + 1) * 16, fh : fh + META] = meta_here
    pl.semaphore_wait(barrier, len(partners))

    sent = []

    def send(src, dst, device):
        i = len(sent)
        copy = pltpu.make_async_remote_copy(
            src_ref=src,
            dst_ref=dst,
            send_sem=send_sem.at[i],
            recv_sem=recv_sem.at[i],
            device_id=device,
            device_id_type=MESH,
        )
        copy.start()
        sent.append(copy)
        return copy

    here = pl.ds(aligned(d, 16), 16)
    first, gather, returns, last = [], {}, [], []
    state = [dict() for _ in CHUNKS]
    seen = []

    def arrived(copy):
        if not any(copy is other for other in seen):
            seen.append(copy)
            copy.wait_recv()

    def d1(_):
        for j in range(1, NX):
            there = pl.ds(aligned(lax.rem(d + j, NX), 16), 16)
            first.append(send(tok.at[there, :], t2.at[0, here, :], at_x(j)))
        t2[0, here, :] = tok[here, :]

    def z0(_):
        for copy in first:
            arrived(copy)
        gather[1] = send(t2.at[0], t2.at[1], at_z(-1))
        gather[-1] = send(t2.at[0], t2.at[NZ - 1], at_z(1))

    def zf(r):
        arrived(gather[r])
        if r > 0:
            gather[r + 1] = send(t2.at[r], t2.at[r + 1], at_z(-1))
        else:
            gather[r - 1] = send(t2.at[NZ + r], t2.at[NZ + r - 1], at_z(1))

    def meta_of(r):
        return sum(
            t2[r % NZ, g * 16 : (g + 1) * 16, fh : fh + META].astype(F32) for g in range(NX)
        )

    def meta_row(meta, row):
        ids = lax.broadcasted_iota(jnp.int32, meta.shape, 0)
        return jnp.sum(jnp.where(ids == row, meta, 0.0), axis=0, keepdims=True)[:, :64]

    slot = lax.broadcasted_iota(jnp.int32, (ROWS, 64), 0)
    lane = lax.broadcasted_iota(jnp.int32, (ROWS, 64), 1)
    group = (
        (slot >= CAP).astype(jnp.int32)
        + (slot >= 2 * CAP).astype(jnp.int32)
        + (slot >= 3 * CAP).astype(jnp.int32)
    )
    place = (slot - CAP * group + 1).astype(F32)
    same_group = (lane >> 4) == group
    half_of_lane = (lane >> 3) & 1

    def choose(code, h):
        return same_group & (half_of_lane == h) & (code == place)

    t_left = 2 * lax.rem(y + NY - 1, NY) + c
    t_right = 2 * lax.rem(y + 1, NY) + c
    t_far = 2 * lax.rem(y + 2, NY) + c

    def select(k):
        r = CHUNKS[k]
        for copy in first if r == 0 else (gather[r],):
            arrived(copy)
        code = meta_row(meta_of(r), e)
        for h in range(2):
            part = jnp.dot(
                choose(code, h).astype(F32).astype(BF16),
                t2[r % NZ, :, 0:fh],
                preferred_element_type=F32,
            )
            rows[k, t, :, h * fh : (h + 1) * fh] = part.astype(BF16)
        block = rows.at[k, t]
        state[k]["ag"] = [send(block, block, device) for device in (at_y(1), at_y(-1), at_y(2))]
        state[k]["sib"] = [send(block, block, sibling)]

    def pass_on(k, i, there):
        state[k]["ag"][i].wait_recv()
        block = rows.at[k, there]
        state[k]["sib"].append(send(block, block, sibling))

    def gl(k):
        pass_on(k, 0, t_left)

    def gr(k):
        pass_on(k, 1, t_right)

    def ga(k):
        pass_on(k, 2, t_far)

    q_right, q_left = lax.rem(d + 1, NX), lax.rem(d + NX - 1, NX)
    q_far = lax.rem(d + 2, NX)
    half_a, half_b = slice(0, fe // 2), slice(fe // 2, fe)

    def quarter(q):
        return pl.ds(aligned(q, 2 * ROWS), 2 * ROWS)

    def hidden(k):
        for copy in state[k]["sib"]:
            copy.wait_recv()
        if loads[0] is not None:
            loads[0].wait()
            loads[0] = None
        lhs[...] = rows[k].astype(F32).reshape(NT * ROWS, fq).astype(BF16)
        tile = min(256, fe)

        @pl.loop(0, fe // tile)
        def _(n):
            cols = pl.ds(pl.multiple_of(n * tile, tile), tile)
            part = dot_nt(lhs[...], dw[cols, :])
            hp32[k, :, cols] = part
            hp[k, :, cols] = part.astype(BF16)

        far, right, left = quarter(q_far), quarter(q_right), quarter(q_left)
        far_a = send(hp.at[k, far, half_a], xo.at[k, :, half_a], at_x(1))
        far_b = send(hp.at[k, far, half_b], xo.at[k, :, half_b], at_x(-1))
        near_b = send(hp.at[k, right, half_b], xl.at[k, :, half_b], at_x(1))
        near_a = send(hp.at[k, left, half_a], xr.at[k, :, half_a], at_x(-1))
        state[k]["rs"] = (far_a, far_b)
        state[k]["rs2"] = [near_b, near_a]

    def add_far(k, i, to, half, dst, device):
        state[k]["rs"][i].wait_recv()
        hp[k, to, half] = (hp32[k, to, half] + xo[k, :, half].astype(F32)).astype(BF16)
        state[k]["rs2"].append(send(hp.at[k, to, half], dst.at[k, :, half], device))

    def ra(k):
        add_far(k, 0, quarter(q_right), half_a, xl, at_x(1))

    def rb(k):
        add_far(k, 1, quarter(q_left), half_b, xr, at_x(-1))

    def rl(k):
        for copy in state[k]["rs2"]:
            copy.wait_recv()
        mine = quarter(d)
        total = hp32[k, mine, :] + xl[k].astype(F32) + xr[k].astype(F32)
        hf[k, mine, :] = total.astype(BF16)
        block = hf.at[k, mine, :]
        state[k]["hg"] = (send(block, block, at_x(1)), send(block, block, at_x(-1)))
        state[k]["hg2"] = []

    def sa(k):
        state[k]["hg"][0].wait_recv()
        block = hf.at[k, quarter(q_left), half_a]
        state[k]["hg2"].append(send(block, block, at_x(1)))

    def sb(k):
        state[k]["hg"][1].wait_recv()
        block = hf.at[k, quarter(q_right), half_b]
        state[k]["hg2"].append(send(block, block, at_x(-1)))

    def back(k):
        for copy in state[k]["hg2"]:
            copy.wait_recv()
        while len(loads) > 1:
            loads.pop().wait()
        source = lax.rem(e + CHUNKS[k] + NZ, NZ)
        slots = pl.ds(aligned(source, NT * ROWS), NT * ROWS)

        @pl.loop(0, fe // 128)
        def _(n):
            cols = pl.ds(pl.multiple_of(n * 128, 128), 128)
            h = hf[k, :, cols].astype(F32)
            gate = gs[slots, cols].astype(F32)
            up = us[slots, cols].astype(F32)
            s = jax.nn.sigmoid(gate)
            gg[:, cols] = (h * up * s * (1.0 + gate * (1.0 - s))).astype(BF16)
            ug[:, cols] = (h * gate * s).astype(BF16)

        tile = 512 if fq % 512 == 0 else min(256, fq)

        @pl.loop(0, fq // tile)
        def _(n):
            cols = pl.ds(pl.multiple_of(n * tile, tile), tile)
            part = dot_nt(gg[...], gw[cols, :]) + dot_nt(ug[...], uw[cols, :])
            for i in range(NT):
                sg[k, i // 2, i % 2, :, cols] = part[i * ROWS : (i + 1) * ROWS]

        state[k]["pair"] = send(sg.at[k, :, 1 - c], yb.at[k], sibling)

    def sp(k):
        state[k]["pair"].wait_recv()
        state[k]["ys"] = []
        for i in range(1, NY):
            q = lax.rem(y + i, NY)
            pb[k, i - 1] = (sg[k, q, c] + yb[k, q]).astype(BF16)
            state[k]["ys"].append(send(pb.at[k, i - 1], yr.at[k, i - 1], at_y(i)))

    def sl(k):
        for copy in state[k]["ys"]:
            copy.wait_recv()
        total = sg[k, y, c] + yb[k, y]
        for i in range(NY - 1):
            total = total + yr[k, i].astype(F32)
        r = CHUNKS[k]
        if r == 0:
            zr[0] = total
        elif abs(r) >= FAR:
            zs_far[k] = total.astype(BF16)
            returns.append(send(zs_far.at[k], zr_far.at[(-r) % NZ - FAR], at_z(r)))
        else:
            zs[k] = total
            returns.append(send(zs.at[k], zr.at[(-r) % NZ], at_z(r)))

    def end(_):
        meta = meta_of(0)
        mix = [[], []]
        for j in range(NZ):
            x = lax.rem(e + j, NZ)
            code, weight = meta_row(meta, x), meta_row(meta, x + NZ)
            for h in range(2):
                mix[h].append(jnp.where(choose(code, h), weight, 0.0))
        mix = [jnp.concatenate(m, axis=0).astype(BF16) for m in mix]
        for copy in returns:
            copy.wait_recv()

        def combine(h):
            cols = slice(h * fh, (h + 1) * fh)
            value = jnp.concatenate(
                [
                    zr_far[j - FAR, :, cols].astype(F32) if FAR <= j <= NZ - FAR else zr[j, :, cols]
                    for j in range(NZ)
                ],
                axis=0,
            )
            coarse = value.astype(BF16)
            fine = (value - coarse.astype(F32)).astype(BF16)
            dims = (((0,), (0,)), ((), ()))
            return lax.dot_general(mix[h], coarse, dims, preferred_element_type=F32) + lax.dot_general(
                mix[h], fine, dims, preferred_element_type=F32
            )

        fin[...] = (combine(0) + combine(1)).astype(BF16)
        for j in range(1, NX):
            there = pl.ds(aligned(lax.rem(d + j, NX), 16), 16)
            last.append(send(fin.at[there, :], fr.at[here, :], at_x(j)))
        fr[here, :] = fin[here, :]

    def finish(_):
        for copy in last:
            copy.wait_recv()
        for q in range(NX):
            both = fr[q * 16 : (q + 1) * 16, :].astype(F32)
            for h in range(2):
                cols = slice((2 * q + h) * fh, (2 * q + h + 1) * fh)
                out[:, cols] = both[h * tokens : (h + 1) * tokens].astype(BF16)

    stages = {
        "d1": d1, "z0": z0, "zf": zf, "select": select, "gl": gl, "gr": gr, "ga": ga,
        "hidden": hidden, "ra": ra, "rb": rb, "rl": rl, "sa": sa, "sb": sb,
        "back": back, "sp": sp, "sl": sl, "end": end, "fin": finish,
    }
    for name, k in ORDER:
        stages[name](k)
    for copy in sent:
        copy.wait_send()


COPIES = 3 + 7 + 8 * (4 + 3 + 4 + 2 + 2 + 2 + 1 + 3) + 7 + 3


def on_device(
    grad_output, comb_weights, expert_ids, down_weight, gate_weight, up_weight, gate_saved, up_saved
):
    tokens, width = grad_output.shape
    fq = width // NX
    fh = fq // 2
    fe = down_weight.shape[1]
    slots = gate_saved.shape[1]
    n = len(CHUNKS)
    vmem = pltpu.VMEM
    any_space = pl.BlockSpec(memory_space=pl.ANY)
    in_vmem = pl.BlockSpec(memory_space=pltpu.VMEM)
    return pl.pallas_call(
        kernel,
        out_shape=jax.ShapeDtypeStruct((tokens, width), BF16),
        in_specs=[in_vmem] * 3 + [any_space] * 5,
        out_specs=in_vmem,
        scratch_shapes=[
            vmem((fe, fq), BF16),
            vmem((fq, fe), BF16),
            vmem((fq, fe), BF16),
            vmem((slots, fe), BF16),
            vmem((slots, fe), BF16),
            vmem((NX * 16, fh + META), BF16),
            vmem((NZ, 64, fh + META), BF16),
            vmem((n, NT, ROWS, fq), BF16),
            vmem((NT * ROWS, fq), BF16),
            vmem((n, NT * ROWS, fe), F32),
            vmem((n, NT * ROWS, fe), BF16),
            vmem((n, 2 * ROWS, fe), BF16),
            vmem((n, 2 * ROWS, fe), BF16),
            vmem((n, 2 * ROWS, fe), BF16),
            vmem((n, NT * ROWS, fe), BF16),
            vmem((NT * ROWS, fe), BF16),
            vmem((NT * ROWS, fe), BF16),
            vmem((n, NY, 2, ROWS, fq), F32),
            vmem((n, NY, ROWS, fq), F32),
            vmem((n, NY - 1, ROWS, fq), BF16),
            vmem((n, NY - 1, ROWS, fq), BF16),
            vmem((n, ROWS, fq), F32),
            vmem((NZ, ROWS, fq), F32),
            vmem((n, ROWS, fq), BF16),
            vmem((NZ - 2 * FAR + 1, ROWS, fq), BF16),
            vmem((64, fh), BF16),
            vmem((64, fh), BF16),
            pltpu.SemaphoreType.DMA((5,)),
            pltpu.SemaphoreType.DMA((COPIES,)),
            pltpu.SemaphoreType.DMA((COPIES,)),
        ],
        compiler_params=pltpu.CompilerParams(
            collective_id=0, has_side_effects=True, vmem_limit_bytes=58 * 1024 * 1024
        ),
        cost_estimate=pl.CostEstimate(
            flops=6 * slots * fe * fq, bytes_accessed=12_000_000, transcendentals=slots * fe
        ),
    )(
        grad_output, expert_ids.T, comb_weights.T,
        down_weight[0], gate_weight[0], up_weight[0], gate_saved[0], up_saved[0],
    )


def solution(mesh):
    in_specs = (
        P(("dp", "expert", "etp"), None),
        P(("dp", "expert", "etp"), None),
        P(("dp", "expert", "etp"), None),
        P("expert", "etp", "dp"),
        P("expert", "dp", "etp"),
        P("expert", "dp", "etp"),
        P("expert", None, "etp"),
        P("expert", None, "etp"),
    )
    return jax.shard_map(
        on_device,
        mesh=mesh,
        in_specs=in_specs,
        out_specs=P(("dp", "expert", "etp"), None),
        check_vma=False,
    )
```

```python
import jax
import jax.numpy as jnp
from jax import lax
from jax.experimental import pallas as pl
from jax.experimental.pallas import tpu as pltpu
from jax.sharding import PartitionSpec as P

MESH = pl.DeviceIdType.MESH
NX, NZ, NT, NY = 4, 8, 8, 4
CAP = 6
ROWS = NX * CAP
META = 128
FAR = 3
CHUNKS = (0, 1, -1, 4, 3, -3, 2, -2)
ORDER = (
    ("d1", 0), ("select", 0), ("z0", 0), ("ga", 0), ("select", 2), ("zf", 1), ("zf", -1),
    ("gl", 0), ("gr", 0), ("select", 1), ("hidden", 0), ("ga", 2), ("select", 6), ("zf", 2),
    ("zf", -2), ("select", 7), ("gl", 2), ("gr", 2), ("ra", 0), ("rb", 0), ("ga", 1),
    ("hidden", 2), ("gl", 1), ("gr", 1), ("rl", 0), ("zf", 3), ("select", 5), ("select", 4),
    ("ga", 6), ("hidden", 1), ("ra", 2), ("rb", 2), ("gl", 6), ("gr", 6), ("ga", 7), ("sb", 0),
    ("sa", 0), ("hidden", 6), ("ra", 1), ("rb", 1), ("gl", 7), ("gr", 7), ("select", 3),
    ("rl", 2), ("ga", 5), ("hidden", 7), ("ra", 6), ("rb", 6), ("gl", 5), ("gr", 5), ("back", 0),
    ("ga", 4), ("rl", 1), ("sa", 2), ("gl", 4), ("gr", 4), ("sb", 2), ("hidden", 5), ("ra", 7),
    ("rb", 7), ("sp", 0), ("ga", 3), ("hidden", 4), ("gl", 3), ("gr", 3), ("rl", 6), ("sb", 1),
    ("sa", 1), ("back", 2), ("ra", 5), ("sl", 0), ("rb", 5), ("rl", 7), ("ra", 4), ("rb", 4),
    ("hidden", 3), ("sp", 2), ("sb", 6), ("sa", 6), ("back", 1), ("sa", 7), ("sb", 7), ("rl", 5),
    ("rl", 4), ("sl", 2), ("rb", 3), ("ra", 3), ("sp", 1), ("back", 6), ("sa", 5), ("sb", 5),
    ("back", 7), ("sp", 6), ("sl", 1), ("sa", 4), ("sb", 4), ("rl", 3), ("back", 5), ("sp", 7),
    ("back", 4), ("sp", 5), ("sl", 6), ("sa", 3), ("sb", 3), ("sp", 4), ("sl", 7), ("back", 3),
    ("sl", 5), ("sp", 3), ("sl", 4), ("sl", 3), ("end", 0), ("fin", 0),
)
F32, BF16 = jnp.float32, jnp.bfloat16


def dot_nt(a, b):
    return lax.dot_general(a, b, (((1,), (1,)), ((), ())), preferred_element_type=F32)


def aligned(start, unit):
    return pl.multiple_of(start * unit, unit)


def kernel(
    grad, ids, comb, dw_hbm, gw_hbm, uw_hbm, gs_hbm, us_hbm, out,
    dw, gw, uw, gs, us, tok, t2, rows, lhs, hp32, hp, xo, xl, xr, hf, gg, ug, sg, yb, pb, yr, zs, zr, zs_far, zr_far, mixes, fin, fr,
    load_sem, send_sem, recv_sem,
):
    d, e, t = lax.axis_index("dp"), lax.axis_index("expert"), lax.axis_index("etp")
    y, c = lax.div(t, 2), lax.rem(t, 2)
    fq = grad.shape[1] // NX
    fh = fq // 2
    fe = dw.shape[0]

    loads = []
    for i, (src, dst) in enumerate(
        ((dw_hbm, dw), (gs_hbm, gs), (us_hbm, us), (gw_hbm, gw), (uw_hbm, uw))
    ):
        loads.append(pltpu.make_async_copy(src, dst, load_sem.at[i]))
        loads[-1].start()

    def at_x(j):
        return (lax.rem(d + j + NX, NX), e, t)

    def at_y(j):
        return (d, e, 2 * lax.rem(y + j + NY, NY) + c)

    def at_z(j):
        return (d, lax.rem(e + j + NZ, NZ), t)

    sibling = (d, e, 2 * y + 1 - c)

    barrier = pltpu.get_barrier_semaphore()
    partners = [at_x(j) for j in range(1, NX)] + [at_z(j) for j in range(1, NZ)]
    partners += [at_y(j) for j in range(1, NY)] + [sibling]
    for device in partners:
        pl.semaphore_signal(barrier, inc=1, device_id=device, device_id_type=MESH)

    tokens = grad.shape[0]
    experts = lax.broadcasted_iota(jnp.int32, (NZ, tokens), 0)
    choices = [ids[i : i + 1, :] == experts for i in range(ids.shape[0])]
    hits = sum(jnp.where(m, 1.0, 0.0) for m in choices)
    weight = sum(
        jnp.where(m, comb[i : i + 1, :].astype(F32), 0.0) for i, m in enumerate(choices)
    )
    earlier = lax.broadcasted_iota(jnp.int32, (tokens, tokens), 0) < lax.broadcasted_iota(
        jnp.int32, (tokens, tokens), 1
    )
    before = jnp.dot(
        hits.astype(BF16), jnp.where(earlier, 1.0, 0.0).astype(BF16), preferred_element_type=F32
    )
    code = jnp.where(hits > 0.0, before + 1.0, 0.0)
    lanes = lax.broadcasted_iota(jnp.int32, (tokens, META), 1)
    token = lax.broadcasted_iota(jnp.int32, (tokens, META), 0)
    spread = jnp.where(((lanes >> 4) == d) & ((lanes & 7) == token), 1.0, 0.0).astype(BF16)
    meta_here = jnp.dot(
        jnp.concatenate([code, weight], axis=0).astype(BF16), spread, preferred_element_type=F32
    ).astype(BF16)
    for q in range(NX):
        parts = [grad[:, (2 * q + h) * fh : (2 * q + h + 1) * fh].astype(F32) for h in range(2)]
        tok[q * 16 : (q + 1) * 16, 0:fh] = jnp.concatenate(parts, axis=0).astype(BF16)
        tok[q * 16 : (q + 1) * 16, fh : fh + META] = meta_here
    pl.semaphore_wait(barrier, len(partners))

    sent = []

    def send(src, dst, device):
        i = len(sent)
        copy = pltpu.make_async_remote_copy(
            src_ref=src,
            dst_ref=dst,
            send_sem=send_sem.at[i],
            recv_sem=recv_sem.at[i],
            device_id=device,
            device_id_type=MESH,
        )
        copy.start()
        sent.append(copy)
        return copy

    here = pl.ds(aligned(d, 16), 16)
    first, gather, returns, last = [], {}, [], []
    state = [dict() for _ in CHUNKS]
    seen = []

    def arrived(copy):
        if not any(copy is other for other in seen):
            seen.append(copy)
            copy.wait_recv()

    def d1(_):
        for j in range(1, NX):
            there = pl.ds(aligned(lax.rem(d + j, NX), 16), 16)
            first.append(send(tok.at[there, :], t2.at[0, here, :], at_x(j)))
        t2[0, here, :] = tok[here, :]

    def z0(_):
        for copy in first:
            arrived(copy)
        gather[1] = send(t2.at[0], t2.at[1], at_z(-1))
        gather[-1] = send(t2.at[0], t2.at[NZ - 1], at_z(1))
        prepare()

    def zf(r):
        arrived(gather[r])
        if r > 0:
            gather[r + 1] = send(t2.at[r], t2.at[r + 1], at_z(-1))
        else:
            gather[r - 1] = send(t2.at[NZ + r], t2.at[NZ + r - 1], at_z(1))

    def meta_of(r):
        return sum(
            t2[r % NZ, g * 16 : (g + 1) * 16, fh : fh + META].astype(F32) for g in range(NX)
        )

    def meta_row(meta, row):
        ids = lax.broadcasted_iota(jnp.int32, meta.shape, 0)
        return jnp.sum(jnp.where(ids == row, meta, 0.0), axis=0, keepdims=True)[:, :64]

    slot = lax.broadcasted_iota(jnp.int32, (ROWS, 64), 0)
    lane = lax.broadcasted_iota(jnp.int32, (ROWS, 64), 1)
    group = (
        (slot >= CAP).astype(jnp.int32)
        + (slot >= 2 * CAP).astype(jnp.int32)
        + (slot >= 3 * CAP).astype(jnp.int32)
    )
    place = (slot - CAP * group + 1).astype(F32)
    same_group = (lane >> 4) == group
    half_of_lane = (lane >> 3) & 1

    def choose(code, h):
        return same_group & (half_of_lane == h) & (code == place)

    t_left = 2 * lax.rem(y + NY - 1, NY) + c
    t_right = 2 * lax.rem(y + 1, NY) + c
    t_far = 2 * lax.rem(y + 2, NY) + c

    def select(k):
        r = CHUNKS[k]
        for copy in first if r == 0 else (gather[r],):
            arrived(copy)
        code = meta_row(meta_of(r), e)
        for h in range(2):
            part = jnp.dot(
                choose(code, h).astype(F32).astype(BF16),
                t2[r % NZ, :, 0:fh],
                preferred_element_type=F32,
            )
            rows[k, t, :, h * fh : (h + 1) * fh] = part.astype(BF16)
        block = rows.at[k, t]
        far = send(block, block, at_y(2))
        state[k]["ag"] = [send(block, block, at_y(1)), send(block, block, at_y(-1)), far]
        state[k]["sib"] = [send(block, block, sibling)]

    def pass_on(k, i, there):
        state[k]["ag"][i].wait_recv()
        block = rows.at[k, there]
        state[k]["sib"].append(send(block, block, sibling))

    def gl(k):
        pass_on(k, 0, t_left)

    def gr(k):
        pass_on(k, 1, t_right)

    def ga(k):
        pass_on(k, 2, t_far)

    q_right, q_left = lax.rem(d + 1, NX), lax.rem(d + NX - 1, NX)
    q_far = lax.rem(d + 2, NX)
    half_a, half_b = slice(0, fe // 2), slice(fe // 2, fe)

    def quarter(q):
        return pl.ds(aligned(q, 2 * ROWS), 2 * ROWS)

    def hidden(k):
        for copy in state[k]["sib"]:
            copy.wait_recv()
        if loads[0] is not None:
            loads[0].wait()
            loads[0] = None
        lhs[...] = rows[k].astype(F32).reshape(NT * ROWS, fq).astype(BF16)
        tile = min(256, fe)

        @pl.loop(0, fe // tile)
        def _(n):
            cols = pl.ds(pl.multiple_of(n * tile, tile), tile)
            part = dot_nt(lhs[...], dw[cols, :])
            hp32[k, :, cols] = part
            hp[k, :, cols] = part.astype(BF16)

        far, right, left = quarter(q_far), quarter(q_right), quarter(q_left)
        far_a = send(hp.at[k, far, half_a], xo.at[k, :, half_a], at_x(1))
        far_b = send(hp.at[k, far, half_b], xo.at[k, :, half_b], at_x(-1))
        near_b = send(hp.at[k, right, half_b], xl.at[k, :, half_b], at_x(1))
        near_a = send(hp.at[k, left, half_a], xr.at[k, :, half_a], at_x(-1))
        state[k]["rs"] = (far_a, far_b)
        state[k]["rs2"] = [near_b, near_a]

    def add_far(k, i, to, half, dst, device):
        state[k]["rs"][i].wait_recv()
        hp[k, to, half] = (hp32[k, to, half] + xo[k, :, half].astype(F32)).astype(BF16)
        state[k]["rs2"].append(send(hp.at[k, to, half], dst.at[k, :, half], device))

    def ra(k):
        add_far(k, 0, quarter(q_right), half_a, xl, at_x(1))

    def rb(k):
        add_far(k, 1, quarter(q_left), half_b, xr, at_x(-1))

    def rl(k):
        for copy in state[k]["rs2"]:
            copy.wait_recv()
        mine = quarter(d)
        total = hp32[k, mine, :] + xl[k].astype(F32) + xr[k].astype(F32)
        hf[k, mine, :] = total.astype(BF16)
        block = hf.at[k, mine, :]
        state[k]["hg"] = (send(block, block, at_x(1)), send(block, block, at_x(-1)))
        state[k]["hg2"] = []

    def sa(k):
        state[k]["hg"][0].wait_recv()
        block = hf.at[k, quarter(q_left), half_a]
        state[k]["hg2"].append(send(block, block, at_x(1)))

    def sb(k):
        state[k]["hg"][1].wait_recv()
        block = hf.at[k, quarter(q_right), half_b]
        state[k]["hg2"].append(send(block, block, at_x(-1)))

    def back(k):
        for copy in state[k]["hg2"]:
            copy.wait_recv()
        while len(loads) > 1:
            loads.pop().wait()
        source = lax.rem(e + CHUNKS[k] + NZ, NZ)
        slots = pl.ds(aligned(source, NT * ROWS), NT * ROWS)

        @pl.loop(0, fe // 128)
        def _(n):
            cols = pl.ds(pl.multiple_of(n * 128, 128), 128)
            h = hf[k, :, cols].astype(F32)
            gate = gs[slots, cols].astype(F32)
            up = us[slots, cols].astype(F32)
            s = jax.nn.sigmoid(gate)
            gg[:, cols] = (h * up * s * (1.0 + gate * (1.0 - s))).astype(BF16)
            ug[:, cols] = (h * gate * s).astype(BF16)

        tile = 512 if fq % 512 == 0 else min(256, fq)
        state[k]["pair"] = []
        for start in range(0, fq, tile):
            cols = slice(start, start + tile)
            part = dot_nt(gg[...], gw[cols, :]) + dot_nt(ug[...], uw[cols, :])
            for i in range(NT):
                sg[k, i // 2, i % 2, :, cols] = part[i * ROWS : (i + 1) * ROWS]
            state[k]["pair"].append(
                send(sg.at[k, :, 1 - c, :, cols], yb.at[k, :, :, cols], sibling)
            )

    def sp(k):
        for copy in state[k]["pair"]:
            copy.wait_recv()
        state[k]["ys"] = []
        for i in (2, 1, 3):
            q = lax.rem(y + i, NY)
            pb[k, i - 1] = (sg[k, q, c] + yb[k, q]).astype(BF16)
            state[k]["ys"].append(send(pb.at[k, i - 1], yr.at[k, i - 1], at_y(i)))

    def sl(k):
        for copy in state[k]["ys"]:
            copy.wait_recv()
        total = sg[k, y, c] + yb[k, y]
        for i in range(NY - 1):
            total = total + yr[k, i].astype(F32)
        r = CHUNKS[k]
        if r == 0:
            zr[0] = total
        elif abs(r) >= FAR:
            zs_far[k] = total.astype(BF16)
            returns.append(send(zs_far.at[k], zr_far.at[(-r) % NZ - FAR], at_z(r)))
        else:
            zs[k] = total
            returns.append(send(zs.at[k], zr.at[(-r) % NZ], at_z(r)))

    def prepare():
        meta = meta_of(0)
        mix = [[], []]
        for j in range(NZ):
            x = lax.rem(e + j, NZ)
            code, weight = meta_row(meta, x), meta_row(meta, x + NZ)
            for h in range(2):
                mix[h].append(jnp.where(choose(code, h), weight, 0.0))
        for h in range(2):
            mixes[h] = jnp.concatenate(mix[h], axis=0).astype(BF16)

    def end(_):
        for copy in returns:
            copy.wait_recv()

        def combine(h):
            cols = slice(h * fh, (h + 1) * fh)
            value = jnp.concatenate(
                [
                    zr_far[j - FAR, :, cols].astype(F32) if FAR <= j <= NZ - FAR else zr[j, :, cols]
                    for j in range(NZ)
                ],
                axis=0,
            )
            coarse = value.astype(BF16)
            fine = (value - coarse.astype(F32)).astype(BF16)
            dims = (((0,), (0,)), ((), ()))
            return lax.dot_general(mixes[h], coarse, dims, preferred_element_type=F32) + lax.dot_general(
                mixes[h], fine, dims, preferred_element_type=F32
            )

        fin[...] = (combine(0) + combine(1)).astype(BF16)
        for j in range(1, NX):
            there = pl.ds(aligned(lax.rem(d + j, NX), 16), 16)
            last.append(send(fin.at[there, :], fr.at[here, :], at_x(j)))
        fr[here, :] = fin[here, :]

    def finish(_):
        for copy in last:
            copy.wait_recv()
        for q in range(NX):
            both = fr[q * 16 : (q + 1) * 16, :].astype(F32)
            for h in range(2):
                cols = slice((2 * q + h) * fh, (2 * q + h + 1) * fh)
                out[:, cols] = both[h * tokens : (h + 1) * tokens].astype(BF16)

    stages = {
        "d1": d1, "z0": z0, "zf": zf, "select": select, "gl": gl, "gr": gr, "ga": ga,
        "hidden": hidden, "ra": ra, "rb": rb, "rl": rl, "sa": sa, "sb": sb,
        "back": back, "sp": sp, "sl": sl, "end": end, "fin": finish,
    }
    for name, k in ORDER:
        stages[name](k)
    for copy in sent:
        copy.wait_send()


COPIES = 3 + 7 + 8 * (4 + 3 + 4 + 2 + 2 + 2 + 3 + 3) + 7 + 3


def on_device(
    grad_output, comb_weights, expert_ids, down_weight, gate_weight, up_weight, gate_saved, up_saved
):
    tokens, width = grad_output.shape
    fq = width // NX
    fh = fq // 2
    fe = down_weight.shape[1]
    slots = gate_saved.shape[1]
    n = len(CHUNKS)
    vmem = pltpu.VMEM
    any_space = pl.BlockSpec(memory_space=pl.ANY)
    in_vmem = pl.BlockSpec(memory_space=pltpu.VMEM)
    return pl.pallas_call(
        kernel,
        out_shape=jax.ShapeDtypeStruct((tokens, width), BF16),
        in_specs=[in_vmem] * 3 + [any_space] * 5,
        out_specs=in_vmem,
        scratch_shapes=[
            vmem((fe, fq), BF16),
            vmem((fq, fe), BF16),
            vmem((fq, fe), BF16),
            vmem((slots, fe), BF16),
            vmem((slots, fe), BF16),
            vmem((NX * 16, fh + META), BF16),
            vmem((NZ, 64, fh + META), BF16),
            vmem((n, NT, ROWS, fq), BF16),
            vmem((NT * ROWS, fq), BF16),
            vmem((n, NT * ROWS, fe), F32),
            vmem((n, NT * ROWS, fe), BF16),
            vmem((n, 2 * ROWS, fe), BF16),
            vmem((n, 2 * ROWS, fe), BF16),
            vmem((n, 2 * ROWS, fe), BF16),
            vmem((n, NT * ROWS, fe), BF16),
            vmem((NT * ROWS, fe), BF16),
            vmem((NT * ROWS, fe), BF16),
            vmem((n, NY, 2, ROWS, fq), F32),
            vmem((n, NY, ROWS, fq), F32),
            vmem((n, NY - 1, ROWS, fq), BF16),
            vmem((n, NY - 1, ROWS, fq), BF16),
            vmem((n, ROWS, fq), F32),
            vmem((NZ, ROWS, fq), F32),
            vmem((n, ROWS, fq), BF16),
            vmem((NZ - 2 * FAR + 1, ROWS, fq), BF16),
            vmem((2, NZ * ROWS, 64), BF16),
            vmem((64, fh), BF16),
            vmem((64, fh), BF16),
            pltpu.SemaphoreType.DMA((5,)),
            pltpu.SemaphoreType.DMA((COPIES,)),
            pltpu.SemaphoreType.DMA((COPIES,)),
        ],
        compiler_params=pltpu.CompilerParams(
            collective_id=0, has_side_effects=True, vmem_limit_bytes=58 * 1024 * 1024
        ),
        cost_estimate=pl.CostEstimate(
            flops=6 * slots * fe * fq, bytes_accessed=12_000_000, transcendentals=slots * fe
        ),
    )(
        grad_output, expert_ids.T, comb_weights.T,
        down_weight[0], gate_weight[0], up_weight[0], gate_saved[0], up_saved[0],
    )


def solution(mesh):
    in_specs = (
        P(("dp", "expert", "etp"), None),
        P(("dp", "expert", "etp"), None),
        P(("dp", "expert", "etp"), None),
        P("expert", "etp", "dp"),
        P("expert", "dp", "etp"),
        P("expert", "dp", "etp"),
        P("expert", None, "etp"),
        P("expert", None, "etp"),
    )
    return jax.shard_map(
        on_device,
        mesh=mesh,
        in_specs=in_specs,
        out_specs=P(("dp", "expert", "etp"), None),
        check_vma=False,
    )
```

```python
import jax
import jax.numpy as jnp
from jax import lax
from jax.experimental import pallas as pl
from jax.experimental.pallas import tpu as pltpu
from jax.sharding import PartitionSpec as P

MESH = pl.DeviceIdType.MESH
NX, NZ, NT, NY = 4, 8, 8, 4
CAP = 6
ROWS = NX * CAP
META = 128
FAR = 3
CHUNKS = (0, 1, -2, 3, 4, -3, 2, -1)
ORDER = (
    ("d1", 0), ("select", 0), ("z0", 0), ("gr", 0), ("gl", 0), ("zf", 1), ("zf", -1),
    ("select", 1), ("select", 7), ("ga", 0), ("hidden", 0), ("gr", 1), ("gl", 1), ("select", 6),
    ("zf", 2), ("zf", -2), ("select", 2), ("ga", 1), ("rb", 0), ("ra", 0), ("gr", 7), ("gl", 7),
    ("hidden", 1), ("ga", 7), ("zf", 3), ("select", 3), ("select", 5), ("gr", 6), ("gl", 6),
    ("rl", 0), ("hidden", 7), ("ra", 1), ("rb", 1), ("ga", 6), ("gl", 2), ("gr", 2),
    ("select", 4), ("sb", 0), ("sa", 0), ("hidden", 6), ("ra", 7), ("rb", 7), ("ga", 2),
    ("gl", 3), ("gr", 3), ("rl", 1), ("hidden", 2), ("ra", 6), ("rb", 6), ("back", 0), ("gr", 5),
    ("gl", 5), ("rl", 7), ("ga", 3), ("sb", 1), ("sa", 1), ("ga", 5), ("ra", 2), ("rb", 2),
    ("gl", 4), ("gr", 4), ("sp", 0), ("rl", 6), ("hidden", 3), ("ga", 4), ("hidden", 5),
    ("sb", 7), ("sa", 7), ("back", 1), ("sb", 6), ("rl", 2), ("sa", 6), ("ra", 3), ("rb", 3),
    ("hidden", 4), ("sl", 0), ("ra", 5), ("rb", 5), ("sp", 1), ("back", 7), ("sb", 2), ("sa", 2),
    ("back", 6), ("rl", 3), ("sp", 7), ("rl", 5), ("ra", 4), ("sl", 1), ("rb", 4), ("back", 2),
    ("sp", 6), ("sb", 3), ("sa", 3), ("sa", 5), ("sb", 5), ("rl", 4), ("sp", 2), ("sl", 7),
    ("back", 3), ("back", 5), ("sb", 4), ("sa", 4), ("sl", 6), ("sp", 3), ("sl", 2), ("sp", 5),
    ("back", 4), ("sl", 3), ("sp", 4), ("sl", 5), ("sl", 4), ("end", 0), ("fin", 0),
)
F32, BF16 = jnp.float32, jnp.bfloat16


def dot_nt(a, b):
    return lax.dot_general(a, b, (((1,), (1,)), ((), ())), preferred_element_type=F32)


def aligned(start, unit):
    return pl.multiple_of(start * unit, unit)


def kernel(
    grad, ids, comb, dw_hbm, gw_hbm, uw_hbm, gs_hbm, us_hbm, out,
    dw, gw, uw, gs, us, tok, t2, rows, lhs, hp32, hp, xo, xl, xr, hf, gg, ug, sg, yb, pb, yr, zs, zr, zs_far, zr_far, mixes, fin, fr,
    load_sem, send_sem, recv_sem,
):
    d, e, t = lax.axis_index("dp"), lax.axis_index("expert"), lax.axis_index("etp")
    y, c = lax.div(t, 2), lax.rem(t, 2)
    fq = grad.shape[1] // NX
    fh = fq // 2
    fe = dw.shape[0]

    loads = []
    for i, (src, dst) in enumerate(
        ((dw_hbm, dw), (gs_hbm, gs), (us_hbm, us), (gw_hbm, gw), (uw_hbm, uw))
    ):
        loads.append(pltpu.make_async_copy(src, dst, load_sem.at[i]))
        loads[-1].start()

    def at_x(j):
        return (lax.rem(d + j + NX, NX), e, t)

    def at_y(j):
        return (d, e, 2 * lax.rem(y + j + NY, NY) + c)

    def at_z(j):
        return (d, lax.rem(e + j + NZ, NZ), t)

    sibling = (d, e, 2 * y + 1 - c)

    barrier = pltpu.get_barrier_semaphore()
    partners = [at_x(j) for j in range(1, NX)] + [at_z(j) for j in range(1, NZ)]
    partners += [at_y(j) for j in range(1, NY)] + [sibling]
    for device in partners:
        pl.semaphore_signal(barrier, inc=1, device_id=device, device_id_type=MESH)

    tokens = grad.shape[0]
    experts = lax.broadcasted_iota(jnp.int32, (NZ, tokens), 0)
    choices = [ids[i : i + 1, :] == experts for i in range(ids.shape[0])]
    hits = sum(jnp.where(m, 1.0, 0.0) for m in choices)
    weight = sum(
        jnp.where(m, comb[i : i + 1, :].astype(F32), 0.0) for i, m in enumerate(choices)
    )
    earlier = lax.broadcasted_iota(jnp.int32, (tokens, tokens), 0) < lax.broadcasted_iota(
        jnp.int32, (tokens, tokens), 1
    )
    before = jnp.dot(
        hits.astype(BF16), jnp.where(earlier, 1.0, 0.0).astype(BF16), preferred_element_type=F32
    )
    code = jnp.where(hits > 0.0, before + 1.0, 0.0)
    lanes = lax.broadcasted_iota(jnp.int32, (tokens, META), 1)
    token = lax.broadcasted_iota(jnp.int32, (tokens, META), 0)
    spread = jnp.where(((lanes >> 4) == d) & ((lanes & 7) == token), 1.0, 0.0).astype(BF16)
    meta_here = jnp.dot(
        jnp.concatenate([code, weight], axis=0).astype(BF16), spread, preferred_element_type=F32
    ).astype(BF16)
    for q in range(NX):
        parts = [grad[:, (2 * q + h) * fh : (2 * q + h + 1) * fh].astype(F32) for h in range(2)]
        tok[q * 16 : (q + 1) * 16, 0:fh] = jnp.concatenate(parts, axis=0).astype(BF16)
        tok[q * 16 : (q + 1) * 16, fh : fh + META] = meta_here
    pl.semaphore_wait(barrier, len(partners))

    sent = []

    def send(src, dst, device):
        i = len(sent)
        copy = pltpu.make_async_remote_copy(
            src_ref=src,
            dst_ref=dst,
            send_sem=send_sem.at[i],
            recv_sem=recv_sem.at[i],
            device_id=device,
            device_id_type=MESH,
        )
        copy.start()
        sent.append(copy)
        return copy

    here = pl.ds(aligned(d, 16), 16)
    first, gather, returns, last = [], {}, [], []
    state = [dict() for _ in CHUNKS]
    seen = []

    def arrived(copy):
        if not any(copy is other for other in seen):
            seen.append(copy)
            copy.wait_recv()

    def d1(_):
        for j in range(1, NX):
            there = pl.ds(aligned(lax.rem(d + j, NX), 16), 16)
            first.append(send(tok.at[there, :], t2.at[0, here, :], at_x(j)))
        t2[0, here, :] = tok[here, :]

    def z0(_):
        for copy in first:
            arrived(copy)
        gather[1] = send(t2.at[0], t2.at[1], at_z(-1))
        gather[-1] = send(t2.at[0], t2.at[NZ - 1], at_z(1))
        prepare()

    def zf(r):
        arrived(gather[r])
        if r > 0:
            gather[r + 1] = send(t2.at[r], t2.at[r + 1], at_z(-1))
        else:
            gather[r - 1] = send(t2.at[NZ + r], t2.at[NZ + r - 1], at_z(1))

    def meta_of(r):
        return sum(
            t2[r % NZ, g * 16 : (g + 1) * 16, fh : fh + META].astype(F32) for g in range(NX)
        )

    def meta_row(meta, row):
        ids = lax.broadcasted_iota(jnp.int32, meta.shape, 0)
        return jnp.sum(jnp.where(ids == row, meta, 0.0), axis=0, keepdims=True)[:, :64]

    slot = lax.broadcasted_iota(jnp.int32, (ROWS, 64), 0)
    lane = lax.broadcasted_iota(jnp.int32, (ROWS, 64), 1)
    group = (
        (slot >= CAP).astype(jnp.int32)
        + (slot >= 2 * CAP).astype(jnp.int32)
        + (slot >= 3 * CAP).astype(jnp.int32)
    )
    place = (slot - CAP * group + 1).astype(F32)
    same_group = (lane >> 4) == group
    half_of_lane = (lane >> 3) & 1

    def choose(code, h):
        return same_group & (half_of_lane == h) & (code == place)

    t_left = 2 * lax.rem(y + NY - 1, NY) + c
    t_right = 2 * lax.rem(y + 1, NY) + c
    t_far = 2 * lax.rem(y + 2, NY) + c

    def select(k):
        r = CHUNKS[k]
        for copy in first if r == 0 else (gather[r],):
            arrived(copy)
        code = meta_row(meta_of(r), e)
        for h in range(2):
            part = jnp.dot(
                choose(code, h).astype(F32).astype(BF16),
                t2[r % NZ, :, 0:fh],
                preferred_element_type=F32,
            )
            rows[k, t, :, h * fh : (h + 1) * fh] = part.astype(BF16)
        block = rows.at[k, t]
        far = send(block, block, at_y(2))
        state[k]["ag"] = [send(block, block, at_y(1)), send(block, block, at_y(-1)), far]
        state[k]["sib"] = [send(block, block, sibling)]

    def pass_on(k, i, there):
        state[k]["ag"][i].wait_recv()
        block = rows.at[k, there]
        state[k]["sib"].append(send(block, block, sibling))

    def gl(k):
        pass_on(k, 0, t_left)

    def gr(k):
        pass_on(k, 1, t_right)

    def ga(k):
        pass_on(k, 2, t_far)

    q_right, q_left = lax.rem(d + 1, NX), lax.rem(d + NX - 1, NX)
    q_far = lax.rem(d + 2, NX)
    half_a, half_b = slice(0, fe // 2), slice(fe // 2, fe)

    def quarter(q):
        return pl.ds(aligned(q, 2 * ROWS), 2 * ROWS)

    def hidden(k):
        for copy in state[k]["sib"]:
            copy.wait_recv()
        if loads[0] is not None:
            loads[0].wait()
            loads[0] = None
        lhs[...] = rows[k].astype(F32).reshape(NT * ROWS, fq).astype(BF16)
        tile = min(256, fe)

        @pl.loop(0, fe // tile)
        def _(n):
            cols = pl.ds(pl.multiple_of(n * tile, tile), tile)
            part = dot_nt(lhs[...], dw[cols, :])
            hp32[k, :, cols] = part
            hp[k, :, cols] = part.astype(BF16)

        far, right, left = quarter(q_far), quarter(q_right), quarter(q_left)
        far_a = send(hp.at[k, far, half_a], xo.at[k, :, half_a], at_x(1))
        far_b = send(hp.at[k, far, half_b], xo.at[k, :, half_b], at_x(-1))
        near_b = send(hp.at[k, right, half_b], xl.at[k, :, half_b], at_x(1))
        near_a = send(hp.at[k, left, half_a], xr.at[k, :, half_a], at_x(-1))
        state[k]["rs"] = (far_a, far_b)
        state[k]["rs2"] = [near_b, near_a]

    def add_far(k, i, to, half, dst, device):
        state[k]["rs"][i].wait_recv()
        hp[k, to, half] = (hp32[k, to, half] + xo[k, :, half].astype(F32)).astype(BF16)
        state[k]["rs2"].append(send(hp.at[k, to, half], dst.at[k, :, half], device))

    def ra(k):
        add_far(k, 0, quarter(q_right), half_a, xl, at_x(1))

    def rb(k):
        add_far(k, 1, quarter(q_left), half_b, xr, at_x(-1))

    def rl(k):
        for copy in state[k]["rs2"]:
            copy.wait_recv()
        mine = quarter(d)
        total = hp32[k, mine, :] + xl[k].astype(F32) + xr[k].astype(F32)
        hf[k, mine, :] = total.astype(BF16)
        block = hf.at[k, mine, :]
        state[k]["hg"] = (send(block, block, at_x(1)), send(block, block, at_x(-1)))
        state[k]["hg2"] = []

    def sa(k):
        state[k]["hg"][0].wait_recv()
        block = hf.at[k, quarter(q_left), half_a]
        state[k]["hg2"].append(send(block, block, at_x(1)))

    def sb(k):
        state[k]["hg"][1].wait_recv()
        block = hf.at[k, quarter(q_right), half_b]
        state[k]["hg2"].append(send(block, block, at_x(-1)))

    def back(k):
        for copy in state[k]["hg2"]:
            copy.wait_recv()
        while len(loads) > 1:
            loads.pop().wait()
        source = lax.rem(e + CHUNKS[k] + NZ, NZ)
        slots = pl.ds(aligned(source, NT * ROWS), NT * ROWS)

        @pl.loop(0, fe // 128)
        def _(n):
            cols = pl.ds(pl.multiple_of(n * 128, 128), 128)
            h = hf[k, :, cols].astype(F32)
            gate = gs[slots, cols].astype(F32)
            up = us[slots, cols].astype(F32)
            s = jax.nn.sigmoid(gate)
            gg[:, cols] = (h * up * s * (1.0 + gate * (1.0 - s))).astype(BF16)
            ug[:, cols] = (h * gate * s).astype(BF16)

        tile = 512 if fq % 512 == 0 else min(256, fq)

        @pl.loop(0, fq // tile)
        def _(n):
            cols = pl.ds(pl.multiple_of(n * tile, tile), tile)
            part = dot_nt(gg[...], gw[cols, :]) + dot_nt(ug[...], uw[cols, :])
            for i in range(NT):
                sg[k, i // 2, i % 2, :, cols] = part[i * ROWS : (i + 1) * ROWS]

        state[k]["pair"] = send(sg.at[k, :, 1 - c], yb.at[k], sibling)

    def sp(k):
        state[k]["pair"].wait_recv()
        state[k]["ys"] = []
        for i in (2, 1, 3):
            q = lax.rem(y + i, NY)
            pb[k, i - 1] = (sg[k, q, c] + yb[k, q]).astype(BF16)
            state[k]["ys"].append(send(pb.at[k, i - 1], yr.at[k, i - 1], at_y(i)))

    def sl(k):
        for copy in state[k]["ys"]:
            copy.wait_recv()
        total = sg[k, y, c] + yb[k, y]
        for i in range(NY - 1):
            total = total + yr[k, i].astype(F32)
        r = CHUNKS[k]
        if r == 0:
            zr[0] = total
        elif abs(r) >= FAR:
            zs_far[k] = total.astype(BF16)
            returns.append(send(zs_far.at[k], zr_far.at[(-r) % NZ - FAR], at_z(r)))
        else:
            zs[k] = total
            returns.append(send(zs.at[k], zr.at[(-r) % NZ], at_z(r)))

    def prepare():
        meta = meta_of(0)
        mix = [[], []]
        for j in range(NZ):
            x = lax.rem(e + j, NZ)
            code, weight = meta_row(meta, x), meta_row(meta, x + NZ)
            for h in range(2):
                mix[h].append(jnp.where(choose(code, h), weight, 0.0))
        for h in range(2):
            mixes[h] = jnp.concatenate(mix[h], axis=0).astype(BF16)

    def end(_):
        for copy in returns:
            copy.wait_recv()

        def combine(h):
            cols = slice(h * fh, (h + 1) * fh)
            value = jnp.concatenate(
                [
                    zr_far[j - FAR, :, cols].astype(F32) if FAR <= j <= NZ - FAR else zr[j, :, cols]
                    for j in range(NZ)
                ],
                axis=0,
            )
            coarse = value.astype(BF16)
            fine = (value - coarse.astype(F32)).astype(BF16)
            dims = (((0,), (0,)), ((), ()))
            return lax.dot_general(mixes[h], coarse, dims, preferred_element_type=F32) + lax.dot_general(
                mixes[h], fine, dims, preferred_element_type=F32
            )

        fin[...] = (combine(0) + combine(1)).astype(BF16)
        for j in range(1, NX):
            there = pl.ds(aligned(lax.rem(d + j, NX), 16), 16)
            last.append(send(fin.at[there, :], fr.at[here, :], at_x(j)))
        fr[here, :] = fin[here, :]

    def finish(_):
        for copy in last:
            copy.wait_recv()
        for q in range(NX):
            both = fr[q * 16 : (q + 1) * 16, :].astype(F32)
            for h in range(2):
                cols = slice((2 * q + h) * fh, (2 * q + h + 1) * fh)
                out[:, cols] = both[h * tokens : (h + 1) * tokens].astype(BF16)

    stages = {
        "d1": d1, "z0": z0, "zf": zf, "select": select, "gl": gl, "gr": gr, "ga": ga,
        "hidden": hidden, "ra": ra, "rb": rb, "rl": rl, "sa": sa, "sb": sb,
        "back": back, "sp": sp, "sl": sl, "end": end, "fin": finish,
    }
    for name, k in ORDER:
        stages[name](k)
    for copy in sent:
        copy.wait_send()


COPIES = 3 + 7 + 8 * (4 + 3 + 4 + 2 + 2 + 2 + 1 + 3) + 7 + 3


def on_device(
    grad_output, comb_weights, expert_ids, down_weight, gate_weight, up_weight, gate_saved, up_saved
):
    tokens, width = grad_output.shape
    fq = width // NX
    fh = fq // 2
    fe = down_weight.shape[1]
    slots = gate_saved.shape[1]
    n = len(CHUNKS)
    vmem = pltpu.VMEM
    any_space = pl.BlockSpec(memory_space=pl.ANY)
    in_vmem = pl.BlockSpec(memory_space=pltpu.VMEM)
    return pl.pallas_call(
        kernel,
        out_shape=jax.ShapeDtypeStruct((tokens, width), BF16),
        in_specs=[in_vmem] * 3 + [any_space] * 5,
        out_specs=in_vmem,
        scratch_shapes=[
            vmem((fe, fq), BF16),
            vmem((fq, fe), BF16),
            vmem((fq, fe), BF16),
            vmem((slots, fe), BF16),
            vmem((slots, fe), BF16),
            vmem((NX * 16, fh + META), BF16),
            vmem((NZ, 64, fh + META), BF16),
            vmem((n, NT, ROWS, fq), BF16),
            vmem((NT * ROWS, fq), BF16),
            vmem((n, NT * ROWS, fe), F32),
            vmem((n, NT * ROWS, fe), BF16),
            vmem((n, 2 * ROWS, fe), BF16),
            vmem((n, 2 * ROWS, fe), BF16),
            vmem((n, 2 * ROWS, fe), BF16),
            vmem((n, NT * ROWS, fe), BF16),
            vmem((NT * ROWS, fe), BF16),
            vmem((NT * ROWS, fe), BF16),
            vmem((n, NY, 2, ROWS, fq), F32),
            vmem((n, NY, ROWS, fq), F32),
            vmem((n, NY - 1, ROWS, fq), BF16),
            vmem((n, NY - 1, ROWS, fq), BF16),
            vmem((n, ROWS, fq), F32),
            vmem((NZ, ROWS, fq), F32),
            vmem((n, ROWS, fq), BF16),
            vmem((NZ - 2 * FAR + 1, ROWS, fq), BF16),
            vmem((2, NZ * ROWS, 64), BF16),
            vmem((64, fh), BF16),
            vmem((64, fh), BF16),
            pltpu.SemaphoreType.DMA((5,)),
            pltpu.SemaphoreType.DMA((COPIES,)),
            pltpu.SemaphoreType.DMA((COPIES,)),
        ],
        compiler_params=pltpu.CompilerParams(
            collective_id=0, has_side_effects=True, vmem_limit_bytes=58 * 1024 * 1024
        ),
        cost_estimate=pl.CostEstimate(
            flops=6 * slots * fe * fq, bytes_accessed=12_000_000, transcendentals=slots * fe
        ),
    )(
        grad_output, expert_ids.T, comb_weights.T,
        down_weight[0], gate_weight[0], up_weight[0], gate_saved[0], up_saved[0],
    )


def solution(mesh):
    in_specs = (
        P(("dp", "expert", "etp"), None),
        P(("dp", "expert", "etp"), None),
        P(("dp", "expert", "etp"), None),
        P("expert", "etp", "dp"),
        P("expert", "dp", "etp"),
        P("expert", "dp", "etp"),
        P("expert", None, "etp"),
        P("expert", None, "etp"),
    )
    return jax.shard_map(
        on_device,
        mesh=mesh,
        in_specs=in_specs,
        out_specs=P(("dp", "expert", "etp"), None),
        check_vma=False,
    )
```

```python
import jax
import jax.numpy as jnp
from jax import lax
from jax.experimental import pallas as pl
from jax.experimental.pallas import tpu as pltpu
from jax.sharding import PartitionSpec as P

MESH = pl.DeviceIdType.MESH
NX, NZ, NT, NY = 4, 8, 8, 4
CAP = 6
ROWS = NX * CAP
META = 128
FAR = 3
CHUNKS = (0, 1, -2, 3, 4, -3, 2, -1)
ORDER = (
    ("d1", 0), ("select", 0), ("z0", 0), ("gr", 0), ("gl", 0), ("zf", 1), ("zf", -1),
    ("select", 1), ("select", 7), ("ga", 0), ("hidden", 0), ("gr", 1), ("gl", 1), ("select", 6),
    ("zf", 2), ("zf", -2), ("select", 2), ("ga", 1), ("rb", 0), ("ra", 0), ("gr", 7), ("gl", 7),
    ("hidden", 1), ("ga", 7), ("zf", 3), ("select", 3), ("select", 5), ("gr", 6), ("gl", 6),
    ("rl", 0), ("hidden", 7), ("ra", 1), ("rb", 1), ("ga", 6), ("gl", 2), ("gr", 2),
    ("select", 4), ("sb", 0), ("sa", 0), ("hidden", 6), ("ra", 7), ("rb", 7), ("ga", 2),
    ("gl", 3), ("gr", 3), ("rl", 1), ("hidden", 2), ("ra", 6), ("rb", 6), ("back", 0), ("gr", 5),
    ("gl", 5), ("rl", 7), ("ga", 3), ("sb", 1), ("sa", 1), ("ga", 5), ("ra", 2), ("rb", 2),
    ("gl", 4), ("gr", 4), ("sp", 0), ("rl", 6), ("hidden", 3), ("ga", 4), ("hidden", 5),
    ("sb", 7), ("sa", 7), ("back", 1), ("sb", 6), ("rl", 2), ("sa", 6), ("ra", 3), ("rb", 3),
    ("hidden", 4), ("sl", 0), ("ra", 5), ("rb", 5), ("sp", 1), ("back", 7), ("sb", 2), ("sa", 2),
    ("back", 6), ("rl", 3), ("sp", 7), ("rl", 5), ("ra", 4), ("sl", 1), ("rb", 4), ("back", 2),
    ("sp", 6), ("sb", 3), ("sa", 3), ("sa", 5), ("sb", 5), ("rl", 4), ("sp", 2), ("sl", 7),
    ("back", 3), ("back", 5), ("sb", 4), ("sa", 4), ("sl", 6), ("sp", 3), ("sl", 2), ("sp", 5),
    ("back", 4), ("sl", 3), ("sp", 4), ("sl", 5), ("sl", 4), ("end", 0), ("fin", 0),
)
F32, BF16 = jnp.float32, jnp.bfloat16


def dot_nt(a, b):
    return lax.dot_general(a, b, (((1,), (1,)), ((), ())), preferred_element_type=F32)


def aligned(start, unit):
    return pl.multiple_of(start * unit, unit)


def kernel(
    grad, ids, comb, dw_hbm, gw_hbm, uw_hbm, gs_hbm, us_hbm, out,
    dw, gw, uw, gs, us, tok, t2, rows, lhs, hp32, hp, xo, xl, xr, hf, gg, ug, sg, yb, pb, yr, zs, zr, zs_far, zr_far, mixes, fin, fr,
    load_sem, send_sem, recv_sem,
):
    d, e, t = lax.axis_index("dp"), lax.axis_index("expert"), lax.axis_index("etp")
    y, c = lax.div(t, 2), lax.rem(t, 2)
    fq = grad.shape[1] // NX
    fh = fq // 2
    fe = dw.shape[0]

    loads = []
    for i, (src, dst) in enumerate(
        ((dw_hbm, dw), (gs_hbm, gs), (us_hbm, us), (gw_hbm, gw), (uw_hbm, uw))
    ):
        loads.append(pltpu.make_async_copy(src, dst, load_sem.at[i]))
        loads[-1].start()

    def at_x(j):
        return (lax.rem(d + j + NX, NX), e, t)

    def at_y(j):
        return (d, e, 2 * lax.rem(y + j + NY, NY) + c)

    def at_z(j):
        return (d, lax.rem(e + j + NZ, NZ), t)

    sibling = (d, e, 2 * y + 1 - c)

    barrier = pltpu.get_barrier_semaphore()
    partners = [at_x(j) for j in range(1, NX)] + [at_z(j) for j in range(1, NZ)]
    partners += [at_y(j) for j in range(1, NY)] + [sibling]
    for device in partners:
        pl.semaphore_signal(barrier, inc=1, device_id=device, device_id_type=MESH)

    tokens = grad.shape[0]
    experts = lax.broadcasted_iota(jnp.int32, (NZ, tokens), 0)
    choices = [ids[i : i + 1, :] == experts for i in range(ids.shape[0])]
    hits = sum(jnp.where(m, 1.0, 0.0) for m in choices)
    weight = sum(
        jnp.where(m, comb[i : i + 1, :].astype(F32), 0.0) for i, m in enumerate(choices)
    )
    earlier = lax.broadcasted_iota(jnp.int32, (tokens, tokens), 0) < lax.broadcasted_iota(
        jnp.int32, (tokens, tokens), 1
    )
    before = jnp.dot(
        hits.astype(BF16), jnp.where(earlier, 1.0, 0.0).astype(BF16), preferred_element_type=F32
    )
    code = jnp.where(hits > 0.0, before + 1.0, 0.0)
    lanes = lax.broadcasted_iota(jnp.int32, (tokens, META), 1)
    token = lax.broadcasted_iota(jnp.int32, (tokens, META), 0)
    spread = jnp.where(((lanes >> 4) == d) & ((lanes & 7) == token), 1.0, 0.0).astype(BF16)
    meta_here = jnp.dot(
        jnp.concatenate([code, weight], axis=0).astype(BF16), spread, preferred_element_type=F32
    ).astype(BF16)
    for q in range(NX):
        parts = [grad[:, (2 * q + h) * fh : (2 * q + h + 1) * fh].astype(F32) for h in range(2)]
        tok[q * 16 : (q + 1) * 16, 0:fh] = jnp.concatenate(parts, axis=0).astype(BF16)
        tok[q * 16 : (q + 1) * 16, fh : fh + META] = meta_here
    pl.semaphore_wait(barrier, len(partners))

    sent = []

    def send(src, dst, device):
        i = len(sent)
        copy = pltpu.make_async_remote_copy(
            src_ref=src,
            dst_ref=dst,
            send_sem=send_sem.at[i],
            recv_sem=recv_sem.at[i],
            device_id=device,
            device_id_type=MESH,
        )
        copy.start()
        sent.append(copy)
        return copy

    here = pl.ds(aligned(d, 16), 16)
    first, gather, returns, last = [], {}, [], []
    state = [dict() for _ in CHUNKS]
    seen = []

    def arrived(copy):
        if not any(copy is other for other in seen):
            seen.append(copy)
            copy.wait_recv()

    def d1(_):
        for j in range(1, NX):
            there = pl.ds(aligned(lax.rem(d + j, NX), 16), 16)
            first.append(send(tok.at[there, :], t2.at[0, here, :], at_x(j)))
        t2[0, here, :] = tok[here, :]

    def z0(_):
        for copy in first:
            arrived(copy)
        gather[1] = send(t2.at[0], t2.at[1], at_z(-1))
        gather[-1] = send(t2.at[0], t2.at[NZ - 1], at_z(1))

    def zf(r):
        arrived(gather[r])
        if r > 0:
            gather[r + 1] = send(t2.at[r], t2.at[r + 1], at_z(-1))
            if r == 2:
                prepare()
        else:
            gather[r - 1] = send(t2.at[NZ + r], t2.at[NZ + r - 1], at_z(1))

    def meta_of(r):
        return sum(
            t2[r % NZ, g * 16 : (g + 1) * 16, fh : fh + META].astype(F32) for g in range(NX)
        )

    def meta_row(meta, row):
        ids = lax.broadcasted_iota(jnp.int32, meta.shape, 0)
        return jnp.sum(jnp.where(ids == row, meta, 0.0), axis=0, keepdims=True)[:, :64]

    slot = lax.broadcasted_iota(jnp.int32, (ROWS, 64), 0)
    lane = lax.broadcasted_iota(jnp.int32, (ROWS, 64), 1)
    group = (
        (slot >= CAP).astype(jnp.int32)
        + (slot >= 2 * CAP).astype(jnp.int32)
        + (slot >= 3 * CAP).astype(jnp.int32)
    )
    place = (slot - CAP * group + 1).astype(F32)
    same_group = (lane >> 4) == group
    half_of_lane = (lane >> 3) & 1

    def choose(code, h):
        return same_group & (half_of_lane == h) & (code == place)

    t_left = 2 * lax.rem(y + NY - 1, NY) + c
    t_right = 2 * lax.rem(y + 1, NY) + c
    t_far = 2 * lax.rem(y + 2, NY) + c

    def select(k):
        r = CHUNKS[k]
        for copy in first if r == 0 else (gather[r],):
            arrived(copy)
        code = meta_row(meta_of(r), e)
        for h in range(2):
            part = jnp.dot(
                choose(code, h).astype(F32).astype(BF16),
                t2[r % NZ, :, 0:fh],
                preferred_element_type=F32,
            )
            rows[k, t, :, h * fh : (h + 1) * fh] = part.astype(BF16)
        block = rows.at[k, t]
        state[k]["ag"] = [send(block, block, device) for device in (at_y(1), at_y(-1), at_y(2))]
        state[k]["sib"] = [send(block, block, sibling)]

    def pass_on(k, i, there):
        state[k]["ag"][i].wait_recv()
        block = rows.at[k, there]
        state[k]["sib"].append(send(block, block, sibling))

    def gl(k):
        pass_on(k, 0, t_left)

    def gr(k):
        pass_on(k, 1, t_right)

    def ga(k):
        pass_on(k, 2, t_far)

    q_right, q_left = lax.rem(d + 1, NX), lax.rem(d + NX - 1, NX)
    q_far = lax.rem(d + 2, NX)
    half_a, half_b = slice(0, fe // 2), slice(fe // 2, fe)

    def quarter(q):
        return pl.ds(aligned(q, 2 * ROWS), 2 * ROWS)

    def hidden(k):
        for copy in state[k]["sib"]:
            copy.wait_recv()
        if loads[0] is not None:
            loads[0].wait()
            loads[0] = None
        lhs[...] = rows[k].astype(F32).reshape(NT * ROWS, fq).astype(BF16)
        tile = min(256, fe)

        @pl.loop(0, fe // tile)
        def _(n):
            cols = pl.ds(pl.multiple_of(n * tile, tile), tile)
            part = dot_nt(lhs[...], dw[cols, :])
            hp32[k, :, cols] = part
            hp[k, :, cols] = part.astype(BF16)

        far, right, left = quarter(q_far), quarter(q_right), quarter(q_left)
        far_a = send(hp.at[k, far, half_a], xo.at[k, :, half_a], at_x(1))
        far_b = send(hp.at[k, far, half_b], xo.at[k, :, half_b], at_x(-1))
        near_b = send(hp.at[k, right, half_b], xl.at[k, :, half_b], at_x(1))
        near_a = send(hp.at[k, left, half_a], xr.at[k, :, half_a], at_x(-1))
        state[k]["rs"] = (far_a, far_b)
        state[k]["rs2"] = [near_b, near_a]

    def add_far(k, i, to, half, dst, device):
        state[k]["rs"][i].wait_recv()
        hp[k, to, half] = (hp32[k, to, half] + xo[k, :, half].astype(F32)).astype(BF16)
        state[k]["rs2"].append(send(hp.at[k, to, half], dst.at[k, :, half], device))

    def ra(k):
        add_far(k, 0, quarter(q_right), half_a, xl, at_x(1))

    def rb(k):
        add_far(k, 1, quarter(q_left), half_b, xr, at_x(-1))

    def rl(k):
        for copy in state[k]["rs2"]:
            copy.wait_recv()
        mine = quarter(d)
        total = hp32[k, mine, :] + xl[k].astype(F32) + xr[k].astype(F32)
        hf[k, mine, :] = total.astype(BF16)
        block = hf.at[k, mine, :]
        state[k]["hg"] = (send(block, block, at_x(1)), send(block, block, at_x(-1)))
        state[k]["hg2"] = []

    def sa(k):
        state[k]["hg"][0].wait_recv()
        block = hf.at[k, quarter(q_left), half_a]
        state[k]["hg2"].append(send(block, block, at_x(1)))

    def sb(k):
        state[k]["hg"][1].wait_recv()
        block = hf.at[k, quarter(q_right), half_b]
        state[k]["hg2"].append(send(block, block, at_x(-1)))

    def back(k):
        for copy in state[k]["hg2"]:
            copy.wait_recv()
        while len(loads) > 1:
            loads.pop().wait()
        source = lax.rem(e + CHUNKS[k] + NZ, NZ)
        slots = pl.ds(aligned(source, NT * ROWS), NT * ROWS)

        @pl.loop(0, fe // 128)
        def _(n):
            cols = pl.ds(pl.multiple_of(n * 128, 128), 128)
            h = hf[k, :, cols].astype(F32)
            gate = gs[slots, cols].astype(F32)
            up = us[slots, cols].astype(F32)
            s = jax.nn.sigmoid(gate)
            gg[:, cols] = (h * up * s * (1.0 + gate * (1.0 - s))).astype(BF16)
            ug[:, cols] = (h * gate * s).astype(BF16)

        tile = 512 if fq % 512 == 0 else min(256, fq)

        @pl.loop(0, fq // tile)
        def _(n):
            cols = pl.ds(pl.multiple_of(n * tile, tile), tile)
            part = dot_nt(gg[...], gw[cols, :]) + dot_nt(ug[...], uw[cols, :])
            for i in range(NT):
                sg[k, i // 2, i % 2, :, cols] = part[i * ROWS : (i + 1) * ROWS]

        state[k]["pair"] = send(sg.at[k, :, 1 - c], yb.at[k], sibling)

    def sp(k):
        state[k]["pair"].wait_recv()
        state[k]["ys"] = []
        for i in range(1, NY):
            q = lax.rem(y + i, NY)
            pb[k, i - 1] = (sg[k, q, c] + yb[k, q]).astype(BF16)
            state[k]["ys"].append(send(pb.at[k, i - 1], yr.at[k, i - 1], at_y(i)))

    def sl(k):
        for copy in state[k]["ys"]:
            copy.wait_recv()
        total = sg[k, y, c] + yb[k, y]
        for i in range(NY - 1):
            total = total + yr[k, i].astype(F32)
        r = CHUNKS[k]
        if r == 0:
            zr[0] = total
        elif abs(r) >= FAR:
            zs_far[k] = total.astype(BF16)
            returns.append(send(zs_far.at[k], zr_far.at[(-r) % NZ - FAR], at_z(r)))
        else:
            zs[k] = total
            returns.append(send(zs.at[k], zr.at[(-r) % NZ], at_z(r)))

    def prepare():
        meta = meta_of(0)
        mix = [[], []]
        for j in range(NZ):
            x = lax.rem(e + j, NZ)
            code, weight = meta_row(meta, x), meta_row(meta, x + NZ)
            for h in range(2):
                mix[h].append(jnp.where(choose(code, h), weight, 0.0))
        for h in range(2):
            mixes[h] = jnp.concatenate(mix[h], axis=0).astype(BF16)

    def end(_):
        for copy in returns:
            copy.wait_recv()

        def combine(h):
            cols = slice(h * fh, (h + 1) * fh)
            value = jnp.concatenate(
                [
                    zr_far[j - FAR, :, cols].astype(F32) if FAR <= j <= NZ - FAR else zr[j, :, cols]
                    for j in range(NZ)
                ],
                axis=0,
            )
            coarse = value.astype(BF16)
            fine = (value - coarse.astype(F32)).astype(BF16)
            dims = (((0,), (0,)), ((), ()))
            return lax.dot_general(mixes[h], coarse, dims, preferred_element_type=F32) + lax.dot_general(
                mixes[h], fine, dims, preferred_element_type=F32
            )

        fin[...] = (combine(0) + combine(1)).astype(BF16)
        for j in range(1, NX):
            there = pl.ds(aligned(lax.rem(d + j, NX), 16), 16)
            last.append(send(fin.at[there, :], fr.at[here, :], at_x(j)))
        fr[here, :] = fin[here, :]

    def finish(_):
        for copy in last:
            copy.wait_recv()
        for q in range(NX):
            both = fr[q * 16 : (q + 1) * 16, :].astype(F32)
            for h in range(2):
                cols = slice((2 * q + h) * fh, (2 * q + h + 1) * fh)
                out[:, cols] = both[h * tokens : (h + 1) * tokens].astype(BF16)

    stages = {
        "d1": d1, "z0": z0, "zf": zf, "select": select, "gl": gl, "gr": gr, "ga": ga,
        "hidden": hidden, "ra": ra, "rb": rb, "rl": rl, "sa": sa, "sb": sb,
        "back": back, "sp": sp, "sl": sl, "end": end, "fin": finish,
    }
    for name, k in ORDER:
        stages[name](k)
    for copy in sent:
        copy.wait_send()


COPIES = 3 + 7 + 8 * (4 + 3 + 4 + 2 + 2 + 2 + 1 + 3) + 7 + 3


def on_device(
    grad_output, comb_weights, expert_ids, down_weight, gate_weight, up_weight, gate_saved, up_saved
):
    tokens, width = grad_output.shape
    fq = width // NX
    fh = fq // 2
    fe = down_weight.shape[1]
    slots = gate_saved.shape[1]
    n = len(CHUNKS)
    vmem = pltpu.VMEM
    any_space = pl.BlockSpec(memory_space=pl.ANY)
    in_vmem = pl.BlockSpec(memory_space=pltpu.VMEM)
    return pl.pallas_call(
        kernel,
        out_shape=jax.ShapeDtypeStruct((tokens, width), BF16),
        in_specs=[in_vmem] * 3 + [any_space] * 5,
        out_specs=in_vmem,
        scratch_shapes=[
            vmem((fe, fq), BF16),
            vmem((fq, fe), BF16),
            vmem((fq, fe), BF16),
            vmem((slots, fe), BF16),
            vmem((slots, fe), BF16),
            vmem((NX * 16, fh + META), BF16),
            vmem((NZ, 64, fh + META), BF16),
            vmem((n, NT, ROWS, fq), BF16),
            vmem((NT * ROWS, fq), BF16),
            vmem((n, NT * ROWS, fe), F32),
            vmem((n, NT * ROWS, fe), BF16),
            vmem((n, 2 * ROWS, fe), BF16),
            vmem((n, 2 * ROWS, fe), BF16),
            vmem((n, 2 * ROWS, fe), BF16),
            vmem((n, NT * ROWS, fe), BF16),
            vmem((NT * ROWS, fe), BF16),
            vmem((NT * ROWS, fe), BF16),
            vmem((n, NY, 2, ROWS, fq), F32),
            vmem((n, NY, ROWS, fq), F32),
            vmem((n, NY - 1, ROWS, fq), BF16),
            vmem((n, NY - 1, ROWS, fq), BF16),
            vmem((n, ROWS, fq), F32),
            vmem((NZ, ROWS, fq), F32),
            vmem((n, ROWS, fq), BF16),
            vmem((NZ - 2 * FAR + 1, ROWS, fq), BF16),
            vmem((2, NZ * ROWS, 64), BF16),
            vmem((64, fh), BF16),
            vmem((64, fh), BF16),
            pltpu.SemaphoreType.DMA((5,)),
            pltpu.SemaphoreType.DMA((COPIES,)),
            pltpu.SemaphoreType.DMA((COPIES,)),
        ],
        compiler_params=pltpu.CompilerParams(
            collective_id=0, has_side_effects=True, vmem_limit_bytes=58 * 1024 * 1024
        ),
        cost_estimate=pl.CostEstimate(
            flops=6 * slots * fe * fq, bytes_accessed=12_000_000, transcendentals=slots * fe
        ),
    )(
        grad_output, expert_ids.T, comb_weights.T,
        down_weight[0], gate_weight[0], up_weight[0], gate_saved[0], up_saved[0],
    )


def solution(mesh):
    in_specs = (
        P(("dp", "expert", "etp"), None),
        P(("dp", "expert", "etp"), None),
        P(("dp", "expert", "etp"), None),
        P("expert", "etp", "dp"),
        P("expert", "dp", "etp"),
        P("expert", "dp", "etp"),
        P("expert", None, "etp"),
        P("expert", None, "etp"),
    )
    return jax.shard_map(
        on_device,
        mesh=mesh,
        in_specs=in_specs,
        out_specs=P(("dp", "expert", "etp"), None),
        check_vma=False,
    )
```
